512 devices in a mesh: dp: 4 (over x_lo, core), seq: 128 (over x_hi, y, z).
Axes of the slice: x: 4 (x_hi: 2, x_lo: 2; x = x_hi * 2 + x_lo), y: 4, z: 16, core: 2. Of those that a mesh axis runs over, the one named last changes fastest.
Arguments:
- features: bfloat16 [32768, 768], P(('dp', 'seq')), parts along dimension 0, may hold values from -6 to 6
- conv_gain: float32 [768], replicated, may hold values from 0.1 to 1.9
- conv_weight: bfloat16 [3840, 768], P('seq'), may hold values from -0.09375 to 0.09375
- attn_gain: float32 [768], replicated, may hold values from 0.1 to 1.9
- query_weight: bfloat16 [768, 1024], replicated, may hold values from -2 to 2
- key_weight: bfloat16 [768, 128], replicated, may hold values from -2 to 2
- value_weight: bfloat16 [768, 192], replicated, may hold values from -0.21875 to 0.21875
Outputs:
- stream: bfloat16 [32768, 768], P(('dp', 'seq')), parts along dimension 0
- attended: bfloat16 [32768, 1536], P(('dp', 'seq')), parts along dimension 0
The draws below stay inside these ranges and needn't reach their ends.
There are 4 independent parts, one for each index of `dp`. The reference program is written for one: setup_inputs(seed, part) draws one part's arguments, and reference() takes and returns one part's arrays. A program takes and returns all parts, laid end to end along the dimension named above; an argument that names none is the same for every part. Nothing has to cross between parts.
All inputs are finite; a program needn't handle non-finite values.
Results may differ from the reference program's by a relative error of at most 0.0075.
Values may be sent and summed in bfloat16 or wider, within the bound.
No kernel may reach another device: no remote copies, remote signals or barrier semaphores. Data moves between devices by JAX's collectives and lax.ppermute only.
A program may use at most 64 MiB of HBM per device.

```python
import math
import jax
import jax.numpy as jnp
from jax import lax

C = 768
H = 8
DK = 128
DV = 192
KW = 5
TOKENS = 8192


def shared_base(key):
    return jax.random.normal(key, (C, DK), jnp.float32) * C ** (-0.5)


def draw_key_weight(key, part):
    base = shared_base(key)
    result = base
    return jnp.clip(result, -2.0, 2.0).astype(jnp.bfloat16)


def draw_query_weight(key, part):
    key = jax.random.fold_in(key, 23)
    noise = jax.random.normal(key, (C, H * DK), jnp.float32) * C ** (-0.5)
    result = noise
    return jnp.clip(result, -2.0, 2.0).astype(jnp.bfloat16)


def steps_of(rng, dims, shards, smallest, high):
    def one(axis_at, parts):
        draws = jax.random.uniform(jax.random.fold_in(jax.random.fold_in(rng, 6), axis_at), (parts,), jnp.float32, smallest / len(shards), high / len(shards))
        return jnp.repeat(jnp.exp(draws), dims[axis_at] // parts).reshape((-1,) + (1,) * (len(dims) - axis_at - 1))

    factor_of = one(*shards[0])
    for cut in shards[1:]:
        factor_of = factor_of * one(*cut)
    return factor_of


def bell_draw(key, dims, scale, most, shards=(), kind=jnp.bfloat16):
    values = scale * jax.random.normal(key, dims, jnp.float32)
    if shards:
        values = values * steps_of(key, dims, shards, -0.22, 0.18)
    return jnp.clip(values, -most, most).astype(kind)


def setup_inputs(seed: int = 0, part: int = 0) -> dict:
    key_of = jax.random.split(jax.random.key(seed), 8)
    part_splits = jax.random.split(jax.random.fold_in(key_of[7], part), 8)
    return {
        "features": bell_draw(part_splits[0], (TOKENS, C), 1.0, 6.0, ((0, 128),)),
        "conv_gain": jnp.clip(1.0 + 0.18 * jax.random.normal(key_of[1], (C,), jnp.float32), 0.1, 1.9),
        "conv_weight": bell_draw(key_of[2], (KW * C, C), (KW * C) ** -0.5, 0.09375, ((0, 128),)),
        "attn_gain": jnp.clip(1.0 + 0.18 * jax.random.normal(key_of[3], (C,), jnp.float32), 0.1, 1.9),
        "query_weight": draw_query_weight(jax.random.fold_in(key_of[7], 71), part),
        "key_weight": draw_key_weight(jax.random.fold_in(key_of[7], 71), part),
        "value_weight": bell_draw(key_of[6], (C, DV), C ** -0.5, 0.21875),
    }


def normalize(values, gain):
    mean_square = lax.optimization_barrier(jnp.mean(values * values, axis=-1, keepdims=True))
    return values * lax.rsqrt(mean_square + 1e-06) * gain

def reference(features, conv_gain, conv_weight, attn_gain, query_weight, key_weight, value_weight):
    inputs = features.astype(jnp.float32)
    activated = jax.nn.gelu(normalize(inputs, conv_gain), approximate=True).astype(jnp.bfloat16)
    padded = jnp.pad(activated, ((KW // 2, KW // 2), (0, 0)))
    conv_out = jnp.zeros((TOKENS, C), jnp.float32)
    for offset in range(KW):
        conv_out = conv_out + jnp.dot(padded[offset:offset + TOKENS], conv_weight[offset * C:(offset + 1) * C], preferred_element_type=jnp.float32)
    stream = (inputs + conv_out).astype(jnp.bfloat16)
    attn_in = normalize(stream.astype(jnp.float32), attn_gain).astype(jnp.bfloat16)
    queries = (jnp.dot(attn_in, query_weight, preferred_element_type=jnp.float32) * DK ** (-0.5)).astype(jnp.bfloat16)
    keys = jnp.dot(attn_in, key_weight, preferred_element_type=jnp.float32).astype(jnp.bfloat16)
    values = jnp.dot(attn_in, value_weight, preferred_element_type=jnp.float32).astype(jnp.bfloat16)
    key_float = keys.astype(jnp.float32)
    value_float = values.astype(jnp.float32)
    block = math.gcd(TOKENS, 512)
    query_blocks = queries.reshape(TOKENS // block, block, H, DK)

    def attend_block(query_block):
        query_float = query_block.astype(jnp.float32)
        scores = jnp.einsum('thd,nd->htn', query_float, key_float)
        largest = lax.optimization_barrier(jnp.max(scores, axis=-1, keepdims=True))
        probs = jnp.exp(scores - largest)
        totals = lax.optimization_barrier(jnp.sum(probs, axis=-1))
        rounded = lax.optimization_barrier(probs.astype(jnp.bfloat16)).astype(jnp.float32)
        weighted = jnp.einsum('htn,ne->hte', rounded, value_float) / totals[..., None]
        return jnp.transpose(weighted, (1, 0, 2)).reshape(block, H * DV).astype(jnp.bfloat16)
    attended = lax.map(attend_block, query_blocks).reshape(TOKENS, H * DV)
    return (stream, attended)
```

```python
import functools

import jax
import jax.numpy as jnp
from jax import lax
from jax.experimental import pallas as pl
from jax.experimental.pallas import tpu as pltpu
from jax.sharding import Mesh
from jax.sharding import PartitionSpec as P

KW = 5
DP = ("xl", "co")
SEQ = ("xh", "y", "zt", "zp")
AXES = DP + SEQ
SIZES = (2, 2, 2, 4, 8, 2)
SHARE = ("xl", "co", "zp")
SPREAD = ("xh", "y")
STATS = 128


def everyone(block, axes, count):
    sent = jnp.broadcast_to(block[None], (count,) + block.shape)
    return lax.all_to_all(sent, axes, 0, 0, tiled=True)


def normalize(values, gain):
    mean_square = jnp.mean(values * values, axis=-1, keepdims=True)
    return values * lax.rsqrt(mean_square + 1e-06) * gain


def attention_kernel(heads, size, x_ref, qw_ref, k_ref, ve_ref, vo_ref, out_ref):
    rows = x_ref.shape[0]
    chunk = 256
    lane = lax.broadcasted_iota(jnp.int32, (chunk, 128), 1)
    scale = size ** (-0.5)
    for start in range(0, rows, chunk):
        part = pl.ds(start, chunk)
        x = x_ref[part, :]
        stats = jnp.zeros((chunk, STATS), jnp.float32)
        for pair in range(heads // 2):
            halves = []
            for odd in range(2):
                head = 2 * pair + odd
                q = jnp.dot(x, qw_ref[:, head * size : (head + 1) * size], preferred_element_type=jnp.float32)
                q = (q * scale).astype(jnp.bfloat16)
                s = lax.dot_general(q, k_ref[...], (((1,), (1,)), ((), ())), preferred_element_type=jnp.float32)
                top = jnp.max(s, axis=-1, keepdims=True)
                p = jnp.exp(s - top).astype(jnp.bfloat16)
                o = jnp.dot(p, (vo_ref if odd else ve_ref)[...], preferred_element_type=jnp.float32)
                total = o[:, 0:1] if odd else o[:, 255:256]
                halves.append(o * (1.0 / total))
                level = top + jnp.log(total)
                first = level.astype(jnp.bfloat16).astype(jnp.float32)
                rest = level - first
                second = rest.astype(jnp.bfloat16).astype(jnp.float32)
                third = rest - second
                stats = jnp.where(lane == head, first, stats)
                stats = jnp.where(lane == 8 + head, second, stats)
                stats = jnp.where(lane == 16 + head, third, stats)
            even, odd = halves
            base = pair * 384
            out_ref[part, base : base + 128] = even[:, :128].astype(jnp.bfloat16)
            out_ref[part, base + 128 : base + 256] = jnp.where(lane < 64, even[:, 128:], odd[:, :128]).astype(jnp.bfloat16)
            out_ref[part, base + 256 : base + 384] = odd[:, 128:].astype(jnp.bfloat16)
        out_ref[part, heads * 192 :] = stats.astype(jnp.bfloat16)


def combine_kernel(heads, parts_ref, out_ref):
    count, rows, _ = parts_ref.shape
    lane = lax.broadcasted_iota(jnp.int32, (rows, 128), 1)
    base = heads * 192
    weights = []
    for head in range(heads):
        levels = []
        for i in range(count):
            stats = parts_ref[i, :, base:].astype(jnp.float32)
            levels.append(stats[:, head : head + 1] + stats[:, 8 + head : 9 + head] + stats[:, 16 + head : 17 + head])
        top = functools.reduce(jnp.maximum, levels)
        shares = [jnp.exp(level - top) for level in levels]
        inverse = 1.0 / functools.reduce(jnp.add, shares)
        weights.append([share * inverse for share in shares])
    for tile in range(heads * 192 // 128):
        low, high = tile * 128 // 192, (tile * 128 + 127) // 192
        total = jnp.zeros((rows, 128), jnp.float32)
        for i in range(count):
            weight = weights[low][i]
            if high != low:
                weight = jnp.where(lane < high * 192 - tile * 128, weight, weights[high][i])
            total = total + weight * parts_ref[i, :, tile * 128 : tile * 128 + 128].astype(jnp.float32)
        out_ref[:, tile * 128 : tile * 128 + 128] = total.astype(jnp.bfloat16)


def local(features, conv_gain, conv_weight, attn_gain, query_weight, key_weight, value_weight):
    rows, width = features.shape
    size = key_weight.shape[1]
    value_size = value_weight.shape[1]
    heads = query_weight.shape[1] // size
    zp = lax.axis_index("zp")
    group = lax.axis_index(DP)
    columns = width // 4

    mine = lax.dynamic_slice_in_dim(conv_weight, group * columns, columns, axis=1)
    blocks = everyone(mine, "zt", 8)
    blocks = everyone(blocks, SPREAD, 8).reshape(64, 1, conv_weight.shape[0], columns)
    empty = jnp.zeros_like(blocks)
    kernel = jnp.concatenate(
        [jnp.where(zp == 0, blocks, empty), jnp.where(zp == 1, blocks, empty)], axis=1
    ).reshape(KW, width, columns)

    edge = jnp.where(zp == 0, features[:2], features[rows - 2 :])
    swaps = [(i, i + 1) for i in range(1, 127, 2)] + [(i + 1, i) for i in range(1, 127, 2)]
    beyond = lax.ppermute(edge, SEQ, swaps)
    inputs = features.astype(jnp.float32)
    extended = jnp.concatenate([inputs, beyond.astype(jnp.float32), jnp.zeros((14, width), jnp.float32)])
    activated = jax.nn.gelu(normalize(extended, conv_gain), approximate=True).astype(jnp.bfloat16)
    shared = everyone(activated, SHARE, 8).reshape(4, 2, rows + 16, width)
    padded = jnp.concatenate(
        [shared[:, 0, rows : rows + 2], shared[:, 0, :rows], shared[:, 1, :rows], shared[:, 1, rows : rows + 2]], axis=1
    )
    windows = jnp.concatenate([padded[:, o : o + 2 * rows] for o in range(KW)], axis=2)
    partial = jnp.dot(
        windows.reshape(8 * rows, KW * width), kernel.reshape(KW * width, columns), preferred_element_type=jnp.float32
    )
    partial = lax.all_to_all(partial.reshape(8, rows, columns), SHARE, 0, 0, tiled=True)
    partial = partial.reshape(4, 2, rows, columns).sum(axis=1)
    conv_out = jnp.concatenate([partial[i] for i in range(4)], axis=1)

    stream = (inputs + conv_out).astype(jnp.bfloat16)
    attn_in = normalize(stream.astype(jnp.float32), attn_gain).astype(jnp.bfloat16)
    both = jnp.concatenate([key_weight, value_weight], axis=1)
    pairs = jnp.dot(attn_in, both, preferred_element_type=jnp.float32).astype(jnp.bfloat16)
    near = everyone(pairs, "zt", 8)
    asked = everyone(attn_in, SPREAD, 8).reshape(8 * rows, width)
    far = lax.ppermute(near, "zp", [(0, 1), (1, 0)])
    pairs = jnp.concatenate([near, far]).reshape(16 * rows, size + value_size)
    keys, values = pairs[:, :size], pairs[:, size:]
    ones = jnp.ones((16 * rows, 256 - value_size), jnp.bfloat16)
    out = pl.pallas_call(
        functools.partial(attention_kernel, heads, size),
        out_shape=jax.ShapeDtypeStruct((8 * rows, heads * value_size + STATS), jnp.bfloat16),
        compiler_params=pltpu.CompilerParams(vmem_limit_bytes=48 * 1024 * 1024),
        name="attention",
    )(asked, query_weight, keys, jnp.concatenate([values, ones], axis=1), jnp.concatenate([ones, values], axis=1))
    parts = lax.all_to_all(out.reshape(8, rows, -1), SPREAD, 0, 0, tiled=True)
    attended = pl.pallas_call(
        functools.partial(combine_kernel, heads),
        out_shape=jax.ShapeDtypeStruct((rows, heads * value_size), jnp.bfloat16),
        compiler_params=pltpu.CompilerParams(vmem_limit_bytes=32 * 1024 * 1024),
        name="combine",
    )(parts)
    return (stream, attended)


def solution(mesh):
    finer = Mesh(mesh.devices.reshape(SIZES), AXES)
    placed = (P(AXES, None), P(), P(SEQ, None), P(), P(), P(), P())
    return jax.shard_map(
        local,
        mesh=finer,
        in_specs=placed,
        out_specs=(P(AXES, None), P(AXES, None)),
        check_vma=False,
    )
```

```python
import functools

import jax
import jax.numpy as jnp
from jax import lax
from jax.experimental import pallas as pl
from jax.experimental.pallas import tpu as pltpu
from jax.sharding import Mesh
from jax.sharding import PartitionSpec as P

KW = 5
DP = ("xl", "co")
SEQ = ("xh", "y1", "y0", "zt", "zp")
AXES = DP + SEQ
SIZES = (2, 2, 2, 2, 2, 8, 2)
SHARE = ("xl", "co", "zp")
WEIGHT = ("xh", "y1", "y0")
COLUMN = ("y1", "y0")
SPREAD = COLUMN + ("zp",)
STATS = 128


def everyone(block, axes, count):
    sent = jnp.broadcast_to(block[None], (count,) + block.shape)
    return lax.all_to_all(sent, axes, 0, 0, tiled=True)


def swapped(block, axis):
    return lax.ppermute(block, axis, [(0, 1), (1, 0)])


def by_masks(block, axes):
    count = 2 ** len(axes)
    return [block] + [
        lax.ppermute(block, axes, [(i, i ^ mask) for i in range(count)]) for mask in range(1, count)
    ]


def normalize(values, gain):
    mean_square = jnp.mean(values * values, axis=-1, keepdims=True)
    return values * lax.rsqrt(mean_square + 1e-06) * gain


def conv_kernel(place_ref, mine_ref, other_ref, end_ref, far_end_ref, w_ref, out_ref, wide_ref):
    group, zp = place_ref[0], place_ref[1]
    parts, rows, width = mine_ref.shape
    count, depth = w_ref.shape[0], KW * width // 128
    wide_ref[...] = jnp.zeros_like(wide_ref)
    for side in range(2):

        @pl.when(zp == side)
        def _():
            for i in range(count):
                start = (2 * i + side) * depth
                block = w_ref[i].astype(jnp.float32)
                tail = block[32:48]
                wide_ref[start : start + depth, :128] = block[:depth]
                wide_ref[start : start + depth // 2, 128:] = tail[: depth // 2]
                wide_ref[start + depth // 2 : start + depth, 128:] = pltpu.roll(tail, 64, 1)[: depth // 2]

    even = zp == 0
    mine, other = mine_ref[...], other_ref[:parts]
    first, second = jnp.where(even, mine, other), jnp.where(even, other, mine)
    x = jnp.concatenate([first, second], axis=1).reshape(2 * parts * rows, width)
    end, far_end = end_ref[...].astype(jnp.float32), far_end_ref[...].astype(jnp.float32)
    before, after = jnp.where(even, end, far_end), jnp.where(even, far_end, end)
    ends = jnp.concatenate([before.reshape(2 * parts, width), after.reshape(2 * parts, width)]).astype(jnp.bfloat16)
    sums = [None] * parts
    for offset in range(KW):
        w = wide_ref[offset * width : (offset + 1) * width, :].astype(jnp.bfloat16)
        y = jnp.dot(x, w, preferred_element_type=jnp.float32)
        z = jnp.dot(ends, w, preferred_element_type=jnp.float32)
        for part in range(parts):
            body = y[2 * part * rows : 2 * (part + 1) * rows]
            before, after = z[2 * part : 2 * part + 2], z[2 * (parts + part) : 2 * (parts + part) + 2]
            term = jnp.concatenate([before, body, after])[offset : offset + 2 * rows]
            sums[part] = term if offset == 0 else sums[part] + term
    for part in range(parts):
        index = jnp.bitwise_xor(group, part)
        value = sums[part][:, : out_ref.shape[2]].astype(jnp.bfloat16)
        out_ref[2 * index] = value
        out_ref[2 * index + 1] = value


def unpack(ref, k_ref, ve_ref, vo_ref):
    lane = lax.broadcasted_iota(jnp.int32, (32, 128), 1)
    one = jnp.ones((32, 128), jnp.float32)
    count = ref.shape[0]
    keys = jnp.concatenate([ref[block, 0:64, :] for block in range(count)])
    k_ref[...] = keys.astype(jnp.float32).T.astype(jnp.bfloat16)
    for block in range(count):
        base = block * 64
        tail = ref[block, 128:160, :].astype(jnp.float32)
        turned = pltpu.roll(tail, 64, 1)
        for half in range(2):
            here = slice(base + 32 * half, base + 32 * half + 32)
            low = ref[block, 64 + 32 * half : 96 + 32 * half, :].astype(jnp.float32)
            shifted = pltpu.roll(low, 64, 1)
            left, right = (turned, tail) if half else (tail, turned)
            ve_ref[here, 0:128] = low.astype(jnp.bfloat16)
            ve_ref[here, 128:256] = jnp.where(lane < 64, left, one).astype(jnp.bfloat16)
            vo_ref[here, 0:128] = jnp.where(lane < 64, one, shifted).astype(jnp.bfloat16)
            vo_ref[here, 128:256] = jnp.where(lane < 64, shifted, right).astype(jnp.bfloat16)


def near_kernel(heads, size, *refs):
    x_refs, (qw_ref, pack_ref, q_ref, o_ref, top_ref, k_ref, ve_ref, vo_ref) = refs[:4], refs[4:]
    unpack(pack_ref, k_ref, ve_ref, vo_ref)
    x = jnp.concatenate([ref[...] for ref in x_refs])
    q = jnp.dot(x, qw_ref[...], preferred_element_type=jnp.float32) * size ** (-0.5)
    q_ref[...] = q.astype(jnp.bfloat16)
    rows, chunk = x.shape[0], 256
    lane = lax.broadcasted_iota(jnp.int32, (chunk, 128), 1)
    for start in range(0, rows, chunk):
        part = slice(start, start + chunk)
        tops = jnp.zeros((chunk, 128), jnp.float32)
        for head in range(heads):
            q = q_ref[part, head * size : (head + 1) * size]
            s = jnp.dot(q, k_ref[...], preferred_element_type=jnp.float32)
            top = jnp.max(s, axis=-1, keepdims=True)
            p = jnp.exp(s - top).astype(jnp.bfloat16)
            v_ref = vo_ref if head % 2 else ve_ref
            o_ref[head, part, :] = jnp.dot(p, v_ref[...], preferred_element_type=jnp.float32)
            tops = jnp.where(lane == head, top, tops)
        top_ref[part, :] = tops


def far_kernel(heads, size, place_ref, q_ref, o_ref, top_ref, pack_ref, out_ref, k_ref, ve_ref, vo_ref):
    unpack(pack_ref, k_ref, ve_ref, vo_ref)
    place = place_ref[0]
    rows, chunk, block = q_ref.shape[0], 256, out_ref.shape[1]
    lane = lax.broadcasted_iota(jnp.int32, (chunk, 128), 1)
    for start in range(0, rows, chunk):
        part = slice(start, start + chunk)
        tops = top_ref[part, :]

        def put(low, value):
            value = value.astype(jnp.bfloat16)
            for i in range(chunk // block):
                at = start // block + i
                index = 2 * jnp.bitwise_xor(place, at // 2) + at % 2
                out_ref[index, :, low : low + 128] = value[i * block : (i + 1) * block]

        stats = jnp.zeros((chunk, STATS), jnp.float32)
        for pair in range(heads // 2):
            halves = []
            for odd in range(2):
                head = 2 * pair + odd
                q = q_ref[part, head * size : (head + 1) * size]
                s = jnp.dot(q, k_ref[...], preferred_element_type=jnp.float32)
                old = tops[:, head : head + 1]
                peak = jnp.maximum(jnp.max(s, axis=-1, keepdims=True), old)
                p = jnp.exp(s - peak).astype(jnp.bfloat16)
                v_ref = vo_ref if odd else ve_ref
                o = jnp.dot(p, v_ref[...], preferred_element_type=jnp.float32)
                o = o + o_ref[head, part, :] * jnp.exp(old - peak)
                halves.append(o)
                if odd:
                    stats = jnp.where(lane == head, o[:, :128], stats)
                else:
                    stats = jnp.where(lane == 64 + head, o[:, 128:], stats)
                stats = jnp.where(lane == 16 + head, peak, stats)
            even, odd = halves
            base = pair * 384
            put(base, even[:, :128])
            put(base + 128, jnp.where(lane < 64, even[:, 128:], odd[:, :128]))
            put(base + 256, odd[:, 128:])
        first = stats.astype(jnp.bfloat16).astype(jnp.float32)
        rest = stats - first
        second = rest.astype(jnp.bfloat16).astype(jnp.float32)
        third = rest - second
        put(heads * 192, first + pltpu.roll(second, 8, 1) + pltpu.roll(third, 32, 1))


def combine_kernel(heads, parts_ref, out_ref):
    count, rows, _ = parts_ref.shape
    lane = lax.broadcasted_iota(jnp.int32, (rows, 128), 1)
    base = heads * 192
    parts = []
    for i in range(count):
        stats = parts_ref[i, :, base:].astype(jnp.float32)
        parts.append(stats + pltpu.roll(stats, STATS - 8, 1) + pltpu.roll(stats, STATS - 32, 1))
    weights = []
    for head in range(heads):
        sum_lane = head if head % 2 else 64 + head
        peaks = [part[:, 16 + head : 17 + head] for part in parts]
        top = functools.reduce(jnp.maximum, peaks)
        scales = [jnp.exp(peak - top) for peak in peaks]
        terms = [part[:, sum_lane : sum_lane + 1] * scale for part, scale in zip(parts, scales)]
        inverse = 1.0 / functools.reduce(jnp.add, terms)
        weights.append([scale * inverse for scale in scales])
    for tile in range(heads * 192 // 128):
        low, high = tile * 128 // 192, (tile * 128 + 127) // 192
        total = jnp.zeros((rows, 128), jnp.float32)
        for i in range(count):
            weight = weights[low][i]
            if high != low:
                weight = jnp.where(lane < high * 192 - tile * 128, weight, weights[high][i])
            total = total + weight * parts_ref[i, :, tile * 128 : tile * 128 + 128].astype(jnp.float32)
        out_ref[:, tile * 128 : tile * 128 + 128] = total.astype(jnp.bfloat16)


def local(features, conv_gain, conv_weight, attn_gain, query_weight, key_weight, value_weight):
    rows, width = features.shape
    size = key_weight.shape[1]
    value_size = value_weight.shape[1]
    heads = query_weight.shape[1] // size
    zp = lax.axis_index("zp")
    group = lax.axis_index(DP)
    columns = width // 4

    half = conv_weight.shape[0] // 2
    whole = lax.dynamic_slice_in_dim(conv_weight, group * 128, 128, axis=1)
    rest = lax.dynamic_slice_in_dim(conv_weight, 512 + group * 64, 64, axis=1)
    rest = jnp.concatenate([rest[:half], rest[half:]], axis=1)
    blocks = everyone(jnp.concatenate([jnp.pad(whole, ((0, 2), (0, 0))), jnp.pad(rest, ((0, 1), (0, 0)))]), "zt", 8)
    shared = by_masks(features, DP)
    blocks, *shared = lax.optimization_barrier((blocks, *shared))

    shared = jnp.stack(shared).astype(jnp.float32)
    activated = jax.nn.gelu(normalize(shared, conv_gain), approximate=True).astype(jnp.bfloat16)
    blocks = everyone(blocks, WEIGHT, 8).reshape(64, 48, 128)
    edge = jnp.where(zp == 0, activated[:, :2], activated[:, rows - 2 :])
    odd, even = range(1, 128, 2), range(0, 128, 2)
    steps = [
        [(i, i + step) for i in odd if i + step < 128] + [(i, i - step) for i in even if i - step >= 0]
        for step in (1, 2)
    ]
    end, far_end = (lax.ppermute(edge, SEQ, step) for step in steps)
    other = swapped(jnp.concatenate([activated, features[None]]), "zp")
    beside = other[4]
    partial = pl.pallas_call(
        conv_kernel,
        out_shape=jax.ShapeDtypeStruct((8, 2 * rows, columns), jnp.bfloat16),
        in_specs=[pl.BlockSpec(memory_space=pltpu.SMEM)] + [pl.BlockSpec(memory_space=pltpu.VMEM)] * 5,
        out_specs=pl.BlockSpec(memory_space=pltpu.VMEM),
        scratch_shapes=[pltpu.VMEM((KW * width, 256), jnp.float32)],
        compiler_params=pltpu.CompilerParams(vmem_limit_bytes=32 * 1024 * 1024),
        name="conv",
    )(jnp.stack([group, zp]), activated, other, end, far_end, blocks)
    partial = lax.all_to_all(partial, SHARE, 0, 0, tiled=True).astype(jnp.float32)
    partial = partial.reshape(4, 2, 2 * rows, columns).sum(axis=1)
    conv_out = jnp.concatenate(
        [partial[i][:, :128] for i in range(4)] + [partial[i][:, 128:] for i in range(4)], axis=1
    )
    mine_first = jnp.concatenate([features, beside])
    other_first = jnp.concatenate([beside, features])
    inputs = jnp.where(zp == 0, mine_first, other_first).astype(jnp.float32)

    wide_stream = (inputs + conv_out).astype(jnp.bfloat16)
    stream = jnp.where(zp == 0, wide_stream[:rows], wide_stream[rows:])
    wide_in = normalize(wide_stream.astype(jnp.float32), attn_gain).astype(jnp.bfloat16)
    attn_in = jnp.where(zp == 0, wide_in[:rows], wide_in[rows:])
    both = jnp.concatenate([key_weight, value_weight], axis=1)
    pairs = jnp.dot(attn_in, both, preferred_element_type=jnp.float32).astype(jnp.bfloat16)
    tail = pairs[:, 256:]
    tail = jnp.concatenate([tail[: rows // 2], tail[rows // 2 :]], axis=1)
    packed = jnp.concatenate([pairs[:, :128], pairs[:, 128:256], tail])
    near = everyone(packed, "zt", 8)
    asked = by_masks(wide_in, COLUMN)
    near, *asked = lax.optimization_barrier((near, *asked))
    far = swapped(near, "xh")
    scratch = [
        pltpu.VMEM((size, 8 * rows), jnp.bfloat16),
        pltpu.VMEM((8 * rows, 256), jnp.bfloat16),
        pltpu.VMEM((8 * rows, 256), jnp.bfloat16),
    ]
    in_vmem = pl.BlockSpec(memory_space=pltpu.VMEM)
    cost = pl.CostEstimate(flops=4_500_000_000, bytes_accessed=8_000_000, transcendentals=2_200_000)
    params = pltpu.CompilerParams(vmem_limit_bytes=32 * 1024 * 1024)
    queries, weighted, tops = pl.pallas_call(
        functools.partial(near_kernel, heads, size),
        out_shape=[
            jax.ShapeDtypeStruct((8 * rows, heads * size), jnp.bfloat16),
            jax.ShapeDtypeStruct((heads, 8 * rows, 256), jnp.float32),
            jax.ShapeDtypeStruct((8 * rows, 128), jnp.float32),
        ],
        in_specs=[in_vmem] * 6,
        out_specs=[in_vmem] * 3,
        scratch_shapes=scratch,
        compiler_params=params,
        cost_estimate=cost,
        name="near",
    )(*asked, query_weight, near)
    out = pl.pallas_call(
        functools.partial(far_kernel, heads, size),
        out_shape=jax.ShapeDtypeStruct((8, rows, heads * value_size + STATS), jnp.bfloat16),
        in_specs=[pl.BlockSpec(memory_space=pltpu.SMEM)] + [in_vmem] * 4,
        out_specs=in_vmem,
        scratch_shapes=scratch,
        compiler_params=params,
        cost_estimate=cost,
        name="far",
    )(lax.axis_index(COLUMN)[None], queries, weighted, tops, far)
    parts = lax.all_to_all(out, SPREAD, 0, 0, tiled=True)
    attended = pl.pallas_call(
        functools.partial(combine_kernel, heads),
        out_shape=jax.ShapeDtypeStruct((rows, heads * value_size), jnp.bfloat16),
        compiler_params=pltpu.CompilerParams(vmem_limit_bytes=32 * 1024 * 1024),
        name="combine",
    )(parts)
    return (stream, attended)


def solution(mesh):
    finer = Mesh(mesh.devices.reshape(SIZES), AXES)
    placed = (P(AXES, None), P(), P(SEQ, None), P(), P(), P(), P())
    return jax.shard_map(
        local,
        mesh=finer,
        in_specs=placed,
        out_specs=(P(AXES, None), P(AXES, None)),
        check_vma=False,
    )
```

```python
import functools

import jax
import jax.numpy as jnp
from jax import lax
from jax.experimental import pallas as pl
from jax.experimental.pallas import tpu as pltpu
from jax.sharding import Mesh
from jax.sharding import PartitionSpec as P

KW = 5
DP = ("xl", "co")
SEQ = ("xh", "y1", "y0", "zt", "zp")
AXES = DP + SEQ
SIZES = (2, 2, 2, 2, 2, 8, 2)
SHARE = ("xl", "co", "zp")
WEIGHT = ("xh", "y1", "y0")
COLUMN = ("y1", "y0")
SPREAD = COLUMN + ("zp",)
STATS = 128


def everyone(block, axes, count):
    sent = jnp.broadcast_to(block[None], (count,) + block.shape)
    return lax.all_to_all(sent, axes, 0, 0, tiled=True)


def swapped(block, axis):
    return lax.ppermute(block, axis, [(0, 1), (1, 0)])


def by_masks(block, axes):
    count = 2 ** len(axes)
    return [block] + [
        lax.ppermute(block, axes, [(i, i ^ mask) for i in range(count)]) for mask in range(1, count)
    ]


def normalize(values, gain):
    mean_square = jnp.mean(values * values, axis=-1, keepdims=True)
    return values * lax.rsqrt(mean_square + 1e-06) * gain


def pack_kernel(w_ref, out_ref):
    group = lax.axis_index(DP)
    depth = w_ref.shape[0]
    whole = w_ref[:, pl.ds(pl.multiple_of(group * 128, 128), 128)].astype(jnp.float32)
    tile = w_ref[:, pl.ds(pl.multiple_of(512 + (group // 2) * 128, 128), 128)].astype(jnp.float32)
    turned = pltpu.roll(tile, 64, 1)
    odd = group % 2 == 1
    left, right = jnp.where(odd, turned, tile), jnp.where(odd, tile, turned)
    half = depth // 2
    lane = lax.broadcasted_iota(jnp.int32, (half, 128), 1)
    rest = jnp.where(lane < 64, left[:half], right[half:])
    out = jnp.concatenate([whole, jnp.zeros((2, 128), jnp.float32), rest, jnp.zeros((1, 128), jnp.float32)])
    out = out.astype(jnp.bfloat16)
    for i in range(out_ref.shape[0]):
        out_ref[i] = out


def activate_kernel(*refs):
    x_refs, (gain_ref, out_ref) = refs[:4], refs[4:]
    for i, ref in enumerate(x_refs):
        values = normalize(ref[...].astype(jnp.float32), gain_ref[...])
        out_ref[i] = jax.nn.gelu(values, approximate=True).astype(jnp.bfloat16)


def conv_kernel(place_ref, mine_ref, other_ref, end_ref, far_end_ref, w_ref, out_ref, wide_ref):
    group, zp = place_ref[0], place_ref[1]
    _, held, width = mine_ref.shape
    rows = 2 * held
    count, depth = w_ref.shape[0], KW * width // 128
    wide_ref[...] = jnp.zeros_like(wide_ref)
    for side in range(2):

        @pl.when(zp == side)
        def _():
            for i in range(count):
                start = (2 * i + side) * depth
                block = w_ref[i].astype(jnp.float32)
                tail = block[32:48]
                wide_ref[start : start + depth, :128] = block[:depth]
                wide_ref[start : start + depth // 2, 128:] = tail[: depth // 2]
                wide_ref[start + depth // 2 : start + depth, 128:] = pltpu.roll(tail, 64, 1)[: depth // 2]

    even = zp == 0
    mine, other = mine_ref[...], other_ref[...]
    first, second = jnp.where(even, mine, other), jnp.where(even, other, mine)
    x = jnp.concatenate([first, second], axis=1).reshape(4 * rows, width)
    end, far_end = end_ref[...].astype(jnp.float32), far_end_ref[...].astype(jnp.float32)
    before, after = jnp.where(even, end, far_end), jnp.where(even, far_end, end)
    ends = jnp.concatenate([before.reshape(8, width), after.reshape(8, width)]).astype(jnp.bfloat16)
    sums = [None] * 4
    for offset in range(KW):
        w = wide_ref[offset * width : (offset + 1) * width, :].astype(jnp.bfloat16)
        y = jnp.dot(x, w, preferred_element_type=jnp.float32)
        z = jnp.dot(ends, w, preferred_element_type=jnp.float32)
        for part in range(4):
            body = y[part * rows : (part + 1) * rows]
            line = jnp.concatenate([z[2 * part : 2 * part + 2], body, z[8 + 2 * part : 10 + 2 * part]])
            term = line[offset : offset + rows]
            sums[part] = term if offset == 0 else sums[part] + term
    lane = lax.broadcasted_iota(jnp.int32, (rows // 2, 128), 1)
    for part in range(4):
        index = jnp.bitwise_xor(group, part)
        whole, rest = sums[part][:, :128], sums[part][:, 128:]
        rest = jnp.where(lane < 64, rest[: rows // 2], pltpu.roll(rest, 64, 1)[rows // 2 :])
        value = jnp.concatenate([whole, rest]).astype(jnp.bfloat16)
        out_ref[2 * index] = value
        out_ref[2 * index + 1] = value


def stream_kernel(place_ref, parts_ref, mine_ref, beside_ref, gain_ref, kw_ref, vw_ref, stream_ref, in_ref, pack_ref):
    even = place_ref[1] == 0
    mine, beside = mine_ref[...].astype(jnp.float32), beside_ref[...].astype(jnp.float32)
    rows = mine.shape[0]
    lane = lax.broadcasted_iota(jnp.int32, (rows, 128), 1)
    wholes, rests = [], []
    for j in range(4):
        total = parts_ref[2 * j].astype(jnp.float32) + parts_ref[2 * j + 1].astype(jnp.float32)
        wholes.append(total[: 2 * rows])
        rests.append((total[2 * rows :], pltpu.roll(total[2 * rows :], 64, 1)))
    tiles = [
        jnp.concatenate(
            [
                jnp.where(lane < 64, rests[j][0], rests[j + 1][1]),
                jnp.where(lane < 64, rests[j][1], rests[j + 1][0]),
            ]
        )
        for j in (0, 2)
    ]
    conv_out = jnp.concatenate(wholes + tiles, axis=1)
    inputs = jnp.concatenate([jnp.where(even, mine, beside), jnp.where(even, beside, mine)])
    stream = (inputs + conv_out).astype(jnp.bfloat16)
    stream_ref[...] = jnp.where(even, stream[:rows], stream[rows:])
    attn_in = normalize(stream.astype(jnp.float32), gain_ref[...]).astype(jnp.bfloat16)
    in_ref[...] = attn_in
    own = jnp.where(even, attn_in[:rows], attn_in[rows:])
    keys = jnp.dot(own, kw_ref[...], preferred_element_type=jnp.float32)
    values = jnp.dot(own, vw_ref[...], preferred_element_type=jnp.float32)
    tail = jnp.concatenate([values[: rows // 2, 128:], values[rows // 2 :, 128:]], axis=1)
    packed = jnp.concatenate([keys, values[:, :128], tail]).astype(jnp.bfloat16)
    for i in range(pack_ref.shape[0]):
        pack_ref[i] = packed


def unpack(ref, k_ref, ve_ref, vo_ref):
    lane = lax.broadcasted_iota(jnp.int32, (32, 128), 1)
    one = jnp.ones((32, 128), jnp.float32)
    count = ref.shape[0]
    keys = jnp.concatenate([ref[block, 0:64, :] for block in range(count)])
    k_ref[...] = keys.astype(jnp.float32).T.astype(jnp.bfloat16)
    for block in range(count):
        base = block * 64
        tail = ref[block, 128:160, :].astype(jnp.float32)
        turned = pltpu.roll(tail, 64, 1)
        for half in range(2):
            here = slice(base + 32 * half, base + 32 * half + 32)
            low = ref[block, 64 + 32 * half : 96 + 32 * half, :].astype(jnp.float32)
            shifted = pltpu.roll(low, 64, 1)
            left, right = (turned, tail) if half else (tail, turned)
            ve_ref[here, 0:128] = low.astype(jnp.bfloat16)
            ve_ref[here, 128:256] = jnp.where(lane < 64, left, one).astype(jnp.bfloat16)
            vo_ref[here, 0:128] = jnp.where(lane < 64, one, shifted).astype(jnp.bfloat16)
            vo_ref[here, 128:256] = jnp.where(lane < 64, shifted, right).astype(jnp.bfloat16)


def near_kernel(heads, size, *refs):
    x_refs, (qw_ref, pack_ref, q_ref, o_ref, top_ref, k_ref, ve_ref, vo_ref) = refs[:4], refs[4:]
    unpack(pack_ref, k_ref, ve_ref, vo_ref)
    x = jnp.concatenate([ref[...] for ref in x_refs])
    q = jnp.dot(x, qw_ref[...], preferred_element_type=jnp.float32) * size ** (-0.5)
    q_ref[...] = q.astype(jnp.bfloat16)
    rows, chunk = x.shape[0], 256
    lane = lax.broadcasted_iota(jnp.int32, (chunk, 128), 1)
    for start in range(0, rows, chunk):
        part = slice(start, start + chunk)
        tops = jnp.zeros((chunk, 128), jnp.float32)
        for head in range(heads):
            q = q_ref[part, head * size : (head + 1) * size]
            s = jnp.dot(q, k_ref[...], preferred_element_type=jnp.float32)
            top = jnp.max(s, axis=-1, keepdims=True)
            p = jnp.exp(s - top).astype(jnp.bfloat16)
            v_ref = vo_ref if head % 2 else ve_ref
            o_ref[head, part, :] = jnp.dot(p, v_ref[...], preferred_element_type=jnp.float32)
            tops = jnp.where(lane == head, top, tops)
        top_ref[part, :] = tops


def far_kernel(heads, size, place_ref, q_ref, o_ref, top_ref, pack_ref, out_ref, k_ref, ve_ref, vo_ref):
    unpack(pack_ref, k_ref, ve_ref, vo_ref)
    place = place_ref[0]
    rows, chunk, block = q_ref.shape[0], 256, out_ref.shape[1]
    lane = lax.broadcasted_iota(jnp.int32, (chunk, 128), 1)
    for start in range(0, rows, chunk):
        part = slice(start, start + chunk)
        tops = top_ref[part, :]

        def put(low, value):
            value = value.astype(jnp.bfloat16)
            for i in range(chunk // block):
                at = start // block + i
                index = 2 * jnp.bitwise_xor(place, at // 2) + at % 2
                out_ref[index, :, low : low + 128] = value[i * block : (i + 1) * block]

        stats = jnp.zeros((chunk, STATS), jnp.float32)
        for pair in range(heads // 2):
            halves = []
            for odd in range(2):
                head = 2 * pair + odd
                q = q_ref[part, head * size : (head + 1) * size]
                s = jnp.dot(q, k_ref[...], preferred_element_type=jnp.float32)
                old = tops[:, head : head + 1]
                peak = jnp.maximum(jnp.max(s, axis=-1, keepdims=True), old)
                p = jnp.exp(s - peak).astype(jnp.bfloat16)
                v_ref = vo_ref if odd else ve_ref
                o = jnp.dot(p, v_ref[...], preferred_element_type=jnp.float32)
                o = o + o_ref[head, part, :] * jnp.exp(old - peak)
                halves.append(o)
                if odd:
                    stats = jnp.where(lane == head, o[:, :128], stats)
                else:
                    stats = jnp.where(lane == 64 + head, o[:, 128:], stats)
                stats = jnp.where(lane == 16 + head, peak, stats)
            even, odd = halves
            base = pair * 384
            put(base, even[:, :128])
            put(base + 128, jnp.where(lane < 64, even[:, 128:], odd[:, :128]))
            put(base + 256, odd[:, 128:])
        first = stats.astype(jnp.bfloat16).astype(jnp.float32)
        rest = stats - first
        second = rest.astype(jnp.bfloat16).astype(jnp.float32)
        third = rest - second
        put(heads * 192, first + pltpu.roll(second, 8, 1) + pltpu.roll(third, 32, 1))


def combine_kernel(heads, parts_ref, out_ref):
    count, rows, _ = parts_ref.shape
    lane = lax.broadcasted_iota(jnp.int32, (rows, 128), 1)
    base = heads * 192
    parts = []
    for i in range(count):
        stats = parts_ref[i, :, base:].astype(jnp.float32)
        parts.append(stats + pltpu.roll(stats, STATS - 8, 1) + pltpu.roll(stats, STATS - 32, 1))
    weights = []
    for head in range(heads):
        sum_lane = head if head % 2 else 64 + head
        peaks = [part[:, 16 + head : 17 + head] for part in parts]
        top = functools.reduce(jnp.maximum, peaks)
        scales = [jnp.exp(peak - top) for peak in peaks]
        terms = [part[:, sum_lane : sum_lane + 1] * scale for part, scale in zip(parts, scales)]
        inverse = 1.0 / functools.reduce(jnp.add, terms)
        weights.append([scale * inverse for scale in scales])
    for tile in range(heads * 192 // 128):
        low, high = tile * 128 // 192, (tile * 128 + 127) // 192
        total = jnp.zeros((rows, 128), jnp.float32)
        for i in range(count):
            weight = weights[low][i]
            if high != low:
                weight = jnp.where(lane < high * 192 - tile * 128, weight, weights[high][i])
            total = total + weight * parts_ref[i, :, tile * 128 : tile * 128 + 128].astype(jnp.float32)
        out_ref[:, tile * 128 : tile * 128 + 128] = total.astype(jnp.bfloat16)


def local(features, conv_gain, conv_weight, attn_gain, query_weight, key_weight, value_weight):
    rows, width = features.shape
    size = key_weight.shape[1]
    value_size = value_weight.shape[1]
    heads = query_weight.shape[1] // size
    zp = lax.axis_index("zp")
    place = jnp.stack([lax.axis_index(DP), zp])
    in_smem = pl.BlockSpec(memory_space=pltpu.SMEM)
    in_vmem = pl.BlockSpec(memory_space=pltpu.VMEM)
    params = pltpu.CompilerParams(vmem_limit_bytes=32 * 1024 * 1024)

    mine = pl.pallas_call(
        pack_kernel,
        out_shape=jax.ShapeDtypeStruct((8, 48, 128), jnp.bfloat16),
        in_specs=[in_vmem],
        out_specs=in_vmem,
        compiler_params=params,
        name="pack",
    )(conv_weight)
    blocks = lax.all_to_all(mine, "zt", 0, 0, tiled=True)

    shared = by_masks(features, DP)
    beside = swapped(features, "zp")
    blocks, beside, *shared = lax.optimization_barrier((blocks, beside, *shared))

    blocks = everyone(blocks, WEIGHT, 8).reshape(64, 48, 128)
    activated = pl.pallas_call(
        activate_kernel,
        out_shape=jax.ShapeDtypeStruct((4, rows, width), jnp.bfloat16),
        in_specs=[in_vmem] * 5,
        out_specs=in_vmem,
        compiler_params=params,
        name="activate",
    )(*shared, conv_gain[None])
    edge = jnp.where(zp == 0, activated[:, :2], activated[:, rows - 2 :])
    odd, even = range(1, 128, 2), range(0, 128, 2)
    steps = [
        [(i, i + step) for i in odd if i + step < 128] + [(i, i - step) for i in even if i - step >= 0]
        for step in (1, 2)
    ]
    other = swapped(activated, "zp")
    end, far_end = (lax.ppermute(edge, SEQ, step) for step in steps)
    partial = pl.pallas_call(
        conv_kernel,
        out_shape=jax.ShapeDtypeStruct((8, 3 * rows, 128), jnp.bfloat16),
        in_specs=[in_smem] + [in_vmem] * 5,
        out_specs=in_vmem,
        scratch_shapes=[pltpu.VMEM((KW * width, 256), jnp.float32)],
        compiler_params=params,
        name="conv",
    )(place, activated, other, end, far_end, blocks)
    partial = lax.all_to_all(partial, SHARE, 0, 0, tiled=True)

    stream, wide_in, packed = pl.pallas_call(
        stream_kernel,
        out_shape=[
            jax.ShapeDtypeStruct((rows, width), jnp.bfloat16),
            jax.ShapeDtypeStruct((2 * rows, width), jnp.bfloat16),
            jax.ShapeDtypeStruct((8, 5 * rows // 2, 128), jnp.bfloat16),
        ],
        in_specs=[in_smem] + [in_vmem] * 6,
        out_specs=[in_vmem] * 3,
        compiler_params=params,
        name="stream",
    )(place, partial, features, beside, attn_gain[None], key_weight, value_weight)
    near = lax.all_to_all(packed, "zt", 0, 0, tiled=True)
    asked = by_masks(wide_in, COLUMN)
    near, *asked = lax.optimization_barrier((near, *asked))
    far = swapped(near, "xh")
    scratch = [
        pltpu.VMEM((size, 8 * rows), jnp.bfloat16),
        pltpu.VMEM((8 * rows, 256), jnp.bfloat16),
        pltpu.VMEM((8 * rows, 256), jnp.bfloat16),
    ]
    cost = pl.CostEstimate(flops=4_500_000_000, bytes_accessed=8_000_000, transcendentals=2_200_000)
    queries, weighted, tops = pl.pallas_call(
        functools.partial(near_kernel, heads, size),
        out_shape=[
            jax.ShapeDtypeStruct((8 * rows, heads * size), jnp.bfloat16),
            jax.ShapeDtypeStruct((heads, 8 * rows, 256), jnp.float32),
            jax.ShapeDtypeStruct((8 * rows, 128), jnp.float32),
        ],
        in_specs=[in_vmem] * 6,
        out_specs=[in_vmem] * 3,
        scratch_shapes=scratch,
        compiler_params=params,
        cost_estimate=cost,
        name="near",
    )(*asked, query_weight, near)
    out = pl.pallas_call(
        functools.partial(far_kernel, heads, size),
        out_shape=jax.ShapeDtypeStruct((8, rows, heads * value_size + STATS), jnp.bfloat16),
        in_specs=[in_smem] + [in_vmem] * 4,
        out_specs=in_vmem,
        scratch_shapes=scratch,
        compiler_params=params,
        cost_estimate=cost,
        name="far",
    )(lax.axis_index(COLUMN)[None], queries, weighted, tops, far)
    parts = lax.all_to_all(out, SPREAD, 0, 0, tiled=True)
    attended = pl.pallas_call(
        functools.partial(combine_kernel, heads),
        out_shape=jax.ShapeDtypeStruct((rows, heads * value_size), jnp.bfloat16),
        compiler_params=pltpu.CompilerParams(vmem_limit_bytes=32 * 1024 * 1024),
        name="combine",
    )(parts)
    return (stream, attended)


def solution(mesh):
    finer = Mesh(mesh.devices.reshape(SIZES), AXES)
    placed = (P(AXES, None), P(), P(SEQ, None), P(), P(), P(), P())
    return jax.shard_map(
        local,
        mesh=finer,
        in_specs=placed,
        out_specs=(P(AXES, None), P(AXES, None)),
        check_vma=False,
    )
```

```python
import functools

import jax
import jax.numpy as jnp
from jax import lax
from jax.experimental import pallas as pl
from jax.experimental.pallas import tpu as pltpu
from jax.sharding import Mesh
from jax.sharding import PartitionSpec as P

KW = 5
DP = ("xl", "co")
SEQ = ("xh", "y1", "y0", "zt", "zp")
AXES = DP + SEQ
SIZES = (2, 2, 2, 2, 2, 8, 2)
SHARE = ("xl", "co", "zp")
SPREAD = ("xh", "y1", "y0")
COLUMN = ("zt", "zp")
STATS = 128


def everyone(block, axes, count):
    sent = jnp.broadcast_to(block[None], (count,) + block.shape)
    return lax.all_to_all(sent, axes, 0, 0, tiled=True)


def swapped(block, axis):
    return lax.ppermute(block, axis, [(0, 1), (1, 0)])


def by_masks(block, axes):
    count = 2 ** len(axes)
    return [block] + [
        lax.ppermute(block, axes, [(i, i ^ mask) for i in range(count)]) for mask in range(1, count)
    ]


def normalize(values, gain):
    mean_square = jnp.mean(values * values, axis=-1, keepdims=True)
    return values * lax.rsqrt(mean_square + 1e-06) * gain


def pack_kernel(w_ref, out_ref):
    group = lax.axis_index(DP)
    depth = w_ref.shape[0]
    whole = w_ref[:, pl.ds(pl.multiple_of(group * 128, 128), 128)].astype(jnp.float32)
    tile = w_ref[:, pl.ds(pl.multiple_of(512 + (group // 2) * 128, 128), 128)].astype(jnp.float32)
    turned = pltpu.roll(tile, 64, 1)
    odd = group % 2 == 1
    left, right = jnp.where(odd, turned, tile), jnp.where(odd, tile, turned)
    half = depth // 2
    lane = lax.broadcasted_iota(jnp.int32, (half, 128), 1)
    rest = jnp.where(lane < 64, left[:half], right[half:])
    out = jnp.concatenate([whole, jnp.zeros((2, 128), jnp.float32), rest, jnp.zeros((1, 128), jnp.float32)])
    out = out.astype(jnp.bfloat16)
    for i in range(out_ref.shape[0]):
        out_ref[i] = out


def activate_kernel(*refs):
    x_refs, (gain_ref, out_ref) = refs[:4], refs[4:]
    for i, ref in enumerate(x_refs):
        values = normalize(ref[...].astype(jnp.float32), gain_ref[...])
        out_ref[i] = jax.nn.gelu(values, approximate=True).astype(jnp.bfloat16)


def conv_kernel(place_ref, mine_ref, other_ref, end_ref, far_end_ref, w_ref, out_ref, wide_ref):
    group, zp = place_ref[0], place_ref[1]
    _, held, width = mine_ref.shape
    rows = 2 * held
    count, depth = w_ref.shape[0], KW * width // 128
    wide_ref[...] = jnp.zeros_like(wide_ref)
    for side in range(2):

        @pl.when(zp == side)
        def _():
            for i in range(count):
                start = (2 * i + side) * depth
                block = w_ref[i].astype(jnp.float32)
                tail = block[32:48]
                wide_ref[start : start + depth, :128] = block[:depth]
                wide_ref[start : start + depth // 2, 128:] = tail[: depth // 2]
                wide_ref[start + depth // 2 : start + depth, 128:] = pltpu.roll(tail, 64, 1)[: depth // 2]

    even = zp == 0
    mine, other = mine_ref[...], other_ref[...]
    first, second = jnp.where(even, mine, other), jnp.where(even, other, mine)
    x = jnp.concatenate([first, second], axis=1).reshape(4 * rows, width)
    end, far_end = end_ref[...].astype(jnp.float32), far_end_ref[...].astype(jnp.float32)
    before, after = jnp.where(even, end, far_end), jnp.where(even, far_end, end)
    ends = jnp.concatenate([before.reshape(8, width), after.reshape(8, width)]).astype(jnp.bfloat16)
    sums = [None] * 4
    for offset in range(KW):
        w = wide_ref[offset * width : (offset + 1) * width, :].astype(jnp.bfloat16)
        y = jnp.dot(x, w, preferred_element_type=jnp.float32)
        z = jnp.dot(ends, w, preferred_element_type=jnp.float32)
        for part in range(4):
            body = y[part * rows : (part + 1) * rows]
            line = jnp.concatenate([z[2 * part : 2 * part + 2], body, z[8 + 2 * part : 10 + 2 * part]])
            term = line[offset : offset + rows]
            sums[part] = term if offset == 0 else sums[part] + term
    lane = lax.broadcasted_iota(jnp.int32, (held // 2, 128), 1)
    for part in range(4):
        index = jnp.bitwise_xor(group, part)
        rest = sums[part][:, 128:]
        turned = pltpu.roll(rest, 64, 1)
        for half in range(2):
            low, middle, high = half * held, half * held + held // 2, (half + 1) * held
            value = [sums[part][low:high, :128], jnp.where(lane < 64, rest[low:middle], turned[middle:high])]
            out_ref[2 * index + half] = jnp.concatenate(value).astype(jnp.bfloat16)


def stream_kernel(parts_ref, mine_ref, gain_ref, kw_ref, vw_ref, stream_ref, in_ref, pack_ref):
    inputs = mine_ref[...].astype(jnp.float32)
    rows = inputs.shape[0]
    lane = lax.broadcasted_iota(jnp.int32, (rows // 2, 128), 1)
    wholes, rests = [], []
    for j in range(4):
        total = parts_ref[2 * j].astype(jnp.float32) + parts_ref[2 * j + 1].astype(jnp.float32)
        wholes.append(total[:rows])
        rests.append((total[rows:], pltpu.roll(total[rows:], 64, 1)))
    tiles = [
        jnp.concatenate(
            [
                jnp.where(lane < 64, rests[j][0], rests[j + 1][1]),
                jnp.where(lane < 64, rests[j][1], rests[j + 1][0]),
            ]
        )
        for j in (0, 2)
    ]
    conv_out = jnp.concatenate(wholes + tiles, axis=1)
    stream = (inputs + conv_out).astype(jnp.bfloat16)
    stream_ref[...] = stream
    attn_in = normalize(stream.astype(jnp.float32), gain_ref[...]).astype(jnp.bfloat16)
    for i in range(in_ref.shape[0]):
        in_ref[i] = attn_in
    keys = jnp.dot(attn_in, kw_ref[...], preferred_element_type=jnp.float32)
    values = jnp.dot(attn_in, vw_ref[...], preferred_element_type=jnp.float32)
    tail = jnp.concatenate([values[: rows // 2, 128:], values[rows // 2 :, 128:]], axis=1)
    pack_ref[...] = jnp.concatenate([keys, values[:, :128], tail]).astype(jnp.bfloat16)


def unpack(ref, k_ref, ve_ref, vo_ref):
    lane = lax.broadcasted_iota(jnp.int32, (32, 128), 1)
    one = jnp.ones((32, 128), jnp.float32)
    count = ref.shape[0]
    keys = jnp.concatenate([ref[block, 0:64, :] for block in range(count)])
    k_ref[...] = keys.astype(jnp.float32).T.astype(jnp.bfloat16)
    for block in range(count):
        base = block * 64
        tail = ref[block, 128:160, :].astype(jnp.float32)
        turned = pltpu.roll(tail, 64, 1)
        for half in range(2):
            here = slice(base + 32 * half, base + 32 * half + 32)
            low = ref[block, 64 + 32 * half : 96 + 32 * half, :].astype(jnp.float32)
            shifted = pltpu.roll(low, 64, 1)
            left, right = (turned, tail) if half else (tail, turned)
            ve_ref[here, 0:128] = low.astype(jnp.bfloat16)
            ve_ref[here, 128:256] = jnp.where(lane < 64, left, one).astype(jnp.bfloat16)
            vo_ref[here, 0:128] = jnp.where(lane < 64, one, shifted).astype(jnp.bfloat16)
            vo_ref[here, 128:256] = jnp.where(lane < 64, shifted, right).astype(jnp.bfloat16)


def attend_kernel(heads, size, x_ref, qw_ref, pack_ref, out_ref, q_ref, k_ref, ve_ref, vo_ref):
    unpack(pack_ref, k_ref, ve_ref, vo_ref)
    blocks, block, width = x_ref.shape
    rows, chunk = blocks * block, 256
    q = jnp.dot(x_ref[...].reshape(rows, width), qw_ref[...], preferred_element_type=jnp.float32) * size ** (-0.5)
    q_ref[...] = q.astype(jnp.bfloat16)
    lane = lax.broadcasted_iota(jnp.int32, (chunk, 128), 1)
    for start in range(0, rows, chunk):
        part = slice(start, start + chunk)

        def put(low, value):
            value = value.astype(jnp.bfloat16)
            for i in range(chunk // block):
                out_ref[start // block + i, :, low : low + 128] = value[i * block : (i + 1) * block]

        stats = jnp.zeros((chunk, STATS), jnp.float32)
        for pair in range(heads // 2):
            halves = []
            for odd in range(2):
                head = 2 * pair + odd
                q = q_ref[part, head * size : (head + 1) * size]
                s = jnp.dot(q, k_ref[...], preferred_element_type=jnp.float32)
                peak = jnp.max(s, axis=-1, keepdims=True)
                p = jnp.exp(s - peak).astype(jnp.bfloat16)
                v_ref = vo_ref if odd else ve_ref
                o = jnp.dot(p, v_ref[...], preferred_element_type=jnp.float32)
                halves.append(o)
                if odd:
                    stats = jnp.where(lane == head, o[:, :128], stats)
                else:
                    stats = jnp.where(lane == 64 + head, o[:, 128:], stats)
                stats = jnp.where(lane == 16 + head, peak, stats)
            even, odd = halves
            base = pair * 384
            put(base, even[:, :128])
            put(base + 128, jnp.where(lane < 64, even[:, 128:], odd[:, :128]))
            put(base + 256, odd[:, 128:])
        first = stats.astype(jnp.bfloat16).astype(jnp.float32)
        rest = stats - first
        second = rest.astype(jnp.bfloat16).astype(jnp.float32)
        third = rest - second
        put(heads * 192, first + pltpu.roll(second, 8, 1) + pltpu.roll(third, 32, 1))


def combine_kernel(heads, parts_ref, out_ref):
    count, rows, _ = parts_ref.shape
    lane = lax.broadcasted_iota(jnp.int32, (rows, 128), 1)
    base = heads * 192
    parts = []
    for i in range(count):
        stats = parts_ref[i, :, base:].astype(jnp.float32)
        parts.append(stats + pltpu.roll(stats, STATS - 8, 1) + pltpu.roll(stats, STATS - 32, 1))
    weights = []
    for head in range(heads):
        sum_lane = head if head % 2 else 64 + head
        peaks = [part[:, 16 + head : 17 + head] for part in parts]
        top = functools.reduce(jnp.maximum, peaks)
        scales = [jnp.exp(peak - top) for peak in peaks]
        terms = [part[:, sum_lane : sum_lane + 1] * scale for part, scale in zip(parts, scales)]
        inverse = 1.0 / functools.reduce(jnp.add, terms)
        weights.append([scale * inverse for scale in scales])
    for tile in range(heads * 192 // 128):
        low, high = tile * 128 // 192, (tile * 128 + 127) // 192
        total = jnp.zeros((rows, 128), jnp.float32)
        for i in range(count):
            weight = weights[low][i]
            if high != low:
                weight = jnp.where(lane < high * 192 - tile * 128, weight, weights[high][i])
            total = total + weight * parts_ref[i, :, tile * 128 : tile * 128 + 128].astype(jnp.float32)
        out_ref[:, tile * 128 : tile * 128 + 128] = total.astype(jnp.bfloat16)


def local(features, conv_gain, conv_weight, attn_gain, query_weight, key_weight, value_weight):
    rows, width = features.shape
    size = key_weight.shape[1]
    value_size = value_weight.shape[1]
    heads = query_weight.shape[1] // size
    zp = lax.axis_index("zp")
    place = jnp.stack([lax.axis_index(DP), zp])
    in_smem = pl.BlockSpec(memory_space=pltpu.SMEM)
    in_vmem = pl.BlockSpec(memory_space=pltpu.VMEM)
    params = pltpu.CompilerParams(vmem_limit_bytes=32 * 1024 * 1024)

    mine = pl.pallas_call(
        pack_kernel,
        out_shape=jax.ShapeDtypeStruct((8, 48, 128), jnp.bfloat16),
        in_specs=[in_vmem],
        out_specs=in_vmem,
        compiler_params=params,
        name="pack",
    )(conv_weight)
    blocks = lax.all_to_all(mine, "zt", 0, 0, tiled=True)

    shared = by_masks(features, DP)
    blocks, *shared = lax.optimization_barrier((blocks, *shared))

    blocks = everyone(blocks, SPREAD, 8).reshape(64, 48, 128)
    activated = pl.pallas_call(
        activate_kernel,
        out_shape=jax.ShapeDtypeStruct((4, rows, width), jnp.bfloat16),
        in_specs=[in_vmem] * 5,
        out_specs=in_vmem,
        compiler_params=params,
        name="activate",
    )(*shared, conv_gain[None])
    edge = jnp.where(zp == 0, activated[:, :2], activated[:, rows - 2 :])
    odd, even = range(1, 128, 2), range(0, 128, 2)
    steps = [
        [(i, i + step) for i in odd if i + step < 128] + [(i, i - step) for i in even if i - step >= 0]
        for step in (1, 2)
    ]
    other = swapped(activated, "zp")
    end, far_end = (lax.ppermute(edge, SEQ, step) for step in steps)
    partial = pl.pallas_call(
        conv_kernel,
        out_shape=jax.ShapeDtypeStruct((8, 3 * rows // 2, 128), jnp.bfloat16),
        in_specs=[in_smem] + [in_vmem] * 5,
        out_specs=in_vmem,
        scratch_shapes=[pltpu.VMEM((KW * width, 256), jnp.float32)],
        compiler_params=params,
        name="conv",
    )(place, activated, other, end, far_end, blocks)
    partial = lax.all_to_all(partial, SHARE, 0, 0, tiled=True)

    stream, attn_in, packed = pl.pallas_call(
        stream_kernel,
        out_shape=[
            jax.ShapeDtypeStruct((rows, width), jnp.bfloat16),
            jax.ShapeDtypeStruct((8, rows, width), jnp.bfloat16),
            jax.ShapeDtypeStruct((5 * rows // 2, 128), jnp.bfloat16),
        ],
        in_specs=[in_vmem] * 5,
        out_specs=[in_vmem] * 3,
        compiler_params=params,
        name="stream",
    )(partial, features, attn_gain[None], key_weight, value_weight)
    asked = lax.all_to_all(attn_in, SPREAD, 0, 0, tiled=True)
    pairs = lax.all_gather(packed, COLUMN, axis=0)
    out = pl.pallas_call(
        functools.partial(attend_kernel, heads, size),
        out_shape=jax.ShapeDtypeStruct((8, rows, heads * value_size + STATS), jnp.bfloat16),
        in_specs=[in_vmem] * 3,
        out_specs=in_vmem,
        scratch_shapes=[
            pltpu.VMEM((8 * rows, heads * size), jnp.bfloat16),
            pltpu.VMEM((size, 16 * rows), jnp.bfloat16),
            pltpu.VMEM((16 * rows, 256), jnp.bfloat16),
            pltpu.VMEM((16 * rows, 256), jnp.bfloat16),
        ],
        compiler_params=params,
        name="attend",
    )(asked, query_weight, pairs)
    parts = lax.all_to_all(out, SPREAD, 0, 0, tiled=True)
    attended = pl.pallas_call(
        functools.partial(combine_kernel, heads),
        out_shape=jax.ShapeDtypeStruct((rows, heads * value_size), jnp.bfloat16),
        compiler_params=pltpu.CompilerParams(vmem_limit_bytes=32 * 1024 * 1024),
        name="combine",
    )(parts)
    return (stream, attended)


def solution(mesh):
    finer = Mesh(mesh.devices.reshape(SIZES), AXES)
    placed = (P(AXES, None), P(), P(SEQ, None), P(), P(), P(), P())
    return jax.shard_map(
        local,
        mesh=finer,
        in_specs=placed,
        out_specs=(P(AXES, None), P(AXES, None)),
        check_vma=False,
    )
```

```python
import functools

import jax
import jax.numpy as jnp
from jax import lax
from jax.experimental import pallas as pl
from jax.experimental.pallas import tpu as pltpu
from jax.sharding import Mesh
from jax.sharding import PartitionSpec as P

KW = 5
DP = ("xl", "co")
SEQ = ("xh", "y1", "y0", "zt", "zp")
AXES = DP + SEQ
SIZES = (2, 2, 2, 2, 2, 8, 2)
SHARE = ("xl", "co", "zp")
SPREAD = ("xh", "y1", "y0")
COLUMN = ("zt", "zp")
STATS = 128


def everyone(block, axes, count):
    sent = jnp.broadcast_to(block[None], (count,) + block.shape)
    return lax.all_to_all(sent, axes, 0, 0, tiled=True)


def swapped(block, axis):
    return lax.ppermute(block, axis, [(0, 1), (1, 0)])


def by_masks(block, axes):
    count = 2 ** len(axes)
    return [block] + [
        lax.ppermute(block, axes, [(i, i ^ mask) for i in range(count)]) for mask in range(1, count)
    ]


def normalize(values, gain):
    mean_square = jnp.mean(values * values, axis=-1, keepdims=True)
    return values * lax.rsqrt(mean_square + 1e-06) * gain


def pack_kernel(w_ref, out_ref):
    group = lax.axis_index(DP)
    depth = w_ref.shape[0]
    whole = w_ref[:, pl.ds(pl.multiple_of(group * 128, 128), 128)].astype(jnp.float32)
    tile = w_ref[:, pl.ds(pl.multiple_of(512 + (group // 2) * 128, 128), 128)].astype(jnp.float32)
    turned = pltpu.roll(tile, 64, 1)
    odd = group % 2 == 1
    left, right = jnp.where(odd, turned, tile), jnp.where(odd, tile, turned)
    half = depth // 2
    lane = lax.broadcasted_iota(jnp.int32, (half, 128), 1)
    rest = jnp.where(lane < 64, left[:half], right[half:])
    out = jnp.concatenate([whole, jnp.zeros((2, 128), jnp.float32), rest, jnp.zeros((1, 128), jnp.float32)])
    out = out.astype(jnp.bfloat16)
    for i in range(out_ref.shape[0]):
        out_ref[i] = out


def activate_kernel(*refs):
    x_refs, (gain_ref, out_ref) = refs[:4], refs[4:]
    for i, ref in enumerate(x_refs):
        values = normalize(ref[...].astype(jnp.float32), gain_ref[...])
        out_ref[i] = jax.nn.gelu(values, approximate=True).astype(jnp.bfloat16)


def expand_kernel(place_ref, w_ref, out_ref, wide_ref):
    zp = place_ref[1]
    count = w_ref.shape[0]
    depth = out_ref.shape[0] // (2 * count)
    wide_ref[...] = jnp.zeros_like(wide_ref)
    for side in range(2):

        @pl.when(zp == side)
        def _():
            for i in range(count):
                start = (2 * i + side) * depth
                block = w_ref[i].astype(jnp.float32)
                tail = block[32:48]
                wide_ref[start : start + depth, :128] = block[:depth]
                wide_ref[start : start + depth // 2, 128:] = tail[: depth // 2]
                wide_ref[start + depth // 2 : start + depth, 128:] = pltpu.roll(tail, 64, 1)[: depth // 2]

    out_ref[...] = wide_ref[...].astype(jnp.bfloat16)


def conv_kernel(place_ref, mine_ref, other_ref, end_ref, far_end_ref, wide_ref, out_ref):
    group, zp = place_ref[0], place_ref[1]
    _, held, width = mine_ref.shape
    rows = 2 * held
    even = zp == 0
    mine, other = mine_ref[...], other_ref[...]
    first, second = jnp.where(even, mine, other), jnp.where(even, other, mine)
    x = jnp.concatenate([first, second], axis=1).reshape(4 * rows, width)
    end, far_end = end_ref[...].astype(jnp.float32), far_end_ref[...].astype(jnp.float32)
    before, after = jnp.where(even, end, far_end), jnp.where(even, far_end, end)
    ends = jnp.concatenate([before.reshape(8, width), after.reshape(8, width)]).astype(jnp.bfloat16)
    sums = [None] * 4
    for offset in range(KW):
        w = wide_ref[offset * width : (offset + 1) * width, :]
        y = jnp.dot(x, w, preferred_element_type=jnp.float32)
        z = jnp.dot(ends, w, preferred_element_type=jnp.float32)
        for part in range(4):
            body = y[part * rows : (part + 1) * rows]
            line = jnp.concatenate([z[2 * part : 2 * part + 2], body, z[8 + 2 * part : 10 + 2 * part]])
            term = line[offset : offset + rows]
            sums[part] = term if offset == 0 else sums[part] + term
    lane = lax.broadcasted_iota(jnp.int32, (held // 2, 128), 1)
    for part in range(4):
        index = jnp.bitwise_xor(group, part)
        rest = sums[part][:, 128:]
        turned = pltpu.roll(rest, 64, 1)
        for half in range(2):
            low, middle, high = half * held, half * held + held // 2, (half + 1) * held
            value = [sums[part][low:high, :128], jnp.where(lane < 64, rest[low:middle], turned[middle:high])]
            out_ref[2 * index + half] = jnp.concatenate(value).astype(jnp.bfloat16)


def stream_kernel(parts_ref, mine_ref, gain_ref, kw_ref, vw_ref, stream_ref, in_ref, pack_ref):
    inputs = mine_ref[...].astype(jnp.float32)
    rows = inputs.shape[0]
    lane = lax.broadcasted_iota(jnp.int32, (rows // 2, 128), 1)
    wholes, rests = [], []
    for j in range(4):
        total = parts_ref[2 * j].astype(jnp.float32) + parts_ref[2 * j + 1].astype(jnp.float32)
        wholes.append(total[:rows])
        rests.append((total[rows:], pltpu.roll(total[rows:], 64, 1)))
    tiles = [
        jnp.concatenate(
            [
                jnp.where(lane < 64, rests[j][0], rests[j + 1][1]),
                jnp.where(lane < 64, rests[j][1], rests[j + 1][0]),
            ]
        )
        for j in (0, 2)
    ]
    conv_out = jnp.concatenate(wholes + tiles, axis=1)
    stream = (inputs + conv_out).astype(jnp.bfloat16)
    stream_ref[...] = stream
    attn_in = normalize(stream.astype(jnp.float32), gain_ref[...]).astype(jnp.bfloat16)
    for i in range(in_ref.shape[0]):
        in_ref[i] = attn_in
    keys = jnp.dot(attn_in, kw_ref[...], preferred_element_type=jnp.float32)
    values = jnp.dot(attn_in, vw_ref[...], preferred_element_type=jnp.float32)
    tail = jnp.concatenate([values[: rows // 2, 128:], values[rows // 2 :, 128:]], axis=1)
    pack_ref[...] = jnp.concatenate([keys, values[:, :128], tail]).astype(jnp.bfloat16)


def unpack(ref, k_ref, ve_ref, vo_ref):
    lane = lax.broadcasted_iota(jnp.int32, (32, 128), 1)
    one = jnp.ones((32, 128), jnp.float32)
    count = ref.shape[0]
    keys = jnp.concatenate([ref[block, 0:64, :] for block in range(count)])
    k_ref[...] = keys.astype(jnp.float32).T.astype(jnp.bfloat16)
    for block in range(count):
        base = block * 64
        tail = ref[block, 128:160, :].astype(jnp.float32)
        turned = pltpu.roll(tail, 64, 1)
        for half in range(2):
            here = slice(base + 32 * half, base + 32 * half + 32)
            low = ref[block, 64 + 32 * half : 96 + 32 * half, :].astype(jnp.float32)
            shifted = pltpu.roll(low, 64, 1)
            left, right = (turned, tail) if half else (tail, turned)
            ve_ref[here, 0:128] = low.astype(jnp.bfloat16)
            ve_ref[here, 128:256] = jnp.where(lane < 64, left, one).astype(jnp.bfloat16)
            vo_ref[here, 0:128] = jnp.where(lane < 64, one, shifted).astype(jnp.bfloat16)
            vo_ref[here, 128:256] = jnp.where(lane < 64, shifted, right).astype(jnp.bfloat16)


def attend_kernel(heads, size, x_ref, qw_ref, pack_ref, out_ref, q_ref, k_ref, ve_ref, vo_ref):
    unpack(pack_ref, k_ref, ve_ref, vo_ref)
    blocks, block, width = x_ref.shape
    rows, chunk = blocks * block, 256
    q = jnp.dot(x_ref[...].reshape(rows, width), qw_ref[...], preferred_element_type=jnp.float32) * size ** (-0.5)
    q_ref[...] = q.astype(jnp.bfloat16)
    lane = lax.broadcasted_iota(jnp.int32, (chunk, 128), 1)
    def scores(start, head):
        q = q_ref[start : start + chunk, head * size : (head + 1) * size]
        return jnp.dot(q, k_ref[...], preferred_element_type=jnp.float32)

    def put(start, low, value):
        value = value.astype(jnp.bfloat16)
        for i in range(chunk // block):
            out_ref[start // block + i, :, low : low + 128] = value[i * block : (i + 1) * block]

    steps = [(start, head) for start in range(0, rows, chunk) for head in range(heads)]
    following = scores(*steps[0])
    for step, (start, head) in enumerate(steps):
        s = following
        if step + 1 < len(steps):
            following = scores(*steps[step + 1])
        peak = jnp.max(s, axis=-1, keepdims=True)
        p = jnp.exp(s - peak).astype(jnp.bfloat16)
        if head == 0:
            stats = jnp.zeros((chunk, STATS), jnp.float32)
        base = head // 2 * 384
        if head % 2 == 0:
            even = jnp.dot(p, ve_ref[...], preferred_element_type=jnp.float32)
            stats = jnp.where(lane == 72 + head, even[:, 128:], stats)
            stats = jnp.where(lane == 64 + head, peak, stats)
            put(start, base, even[:, :128])
        else:
            odd = jnp.dot(p, vo_ref[...], preferred_element_type=jnp.float32)
            stats = jnp.where(lane == 8 + head, odd[:, :128], stats)
            stats = jnp.where(lane == head, peak, stats)
            put(start, base + 128, jnp.where(lane < 64, even[:, 128:], odd[:, :128]))
            put(start, base + 256, odd[:, 128:])
        if head == heads - 1:
            first = stats.astype(jnp.bfloat16).astype(jnp.float32)
            rest = stats - first
            second = rest.astype(jnp.bfloat16).astype(jnp.float32)
            third = rest - second
            put(start, heads * 192, first + pltpu.roll(second, 16, 1) + pltpu.roll(third, 32, 1))


def combine_kernel(heads, parts_ref, out_ref):
    count, rows, _ = parts_ref.shape
    lane = lax.broadcasted_iota(jnp.int32, (rows, 128), 1)
    base = heads * 192
    parts = []
    for i in range(count):
        stats = parts_ref[i, :, base:].astype(jnp.float32)
        parts.append(stats + pltpu.roll(stats, STATS - 16, 1) + pltpu.roll(stats, STATS - 32, 1))
    top = functools.reduce(jnp.maximum, parts)
    scales = [jnp.exp(part - top) for part in parts]
    terms = [scale * pltpu.roll(part, STATS - 8, 1) for part, scale in zip(parts, scales)]
    inverse = 1.0 / functools.reduce(jnp.add, terms)
    shares = [scale * inverse for scale in scales]
    weights = []
    for head in range(heads):
        at = head if head % 2 else 64 + head
        weights.append([share[:, at : at + 1] for share in shares])
    for tile in range(heads * 192 // 128):
        low, high = tile * 128 // 192, (tile * 128 + 127) // 192
        total = jnp.zeros((rows, 128), jnp.float32)
        for i in range(count):
            weight = weights[low][i]
            if high != low:
                weight = jnp.where(lane < high * 192 - tile * 128, weight, weights[high][i])
            total = total + weight * parts_ref[i, :, tile * 128 : tile * 128 + 128].astype(jnp.float32)
        out_ref[:, tile * 128 : tile * 128 + 128] = total.astype(jnp.bfloat16)


def local(features, conv_gain, conv_weight, attn_gain, query_weight, key_weight, value_weight):
    rows, width = features.shape
    size = key_weight.shape[1]
    value_size = value_weight.shape[1]
    heads = query_weight.shape[1] // size
    zp = lax.axis_index("zp")
    place = jnp.stack([lax.axis_index(DP), zp])
    in_smem = pl.BlockSpec(memory_space=pltpu.SMEM)
    in_vmem = pl.BlockSpec(memory_space=pltpu.VMEM)
    params = pltpu.CompilerParams(vmem_limit_bytes=32 * 1024 * 1024)

    mine = pl.pallas_call(
        pack_kernel,
        out_shape=jax.ShapeDtypeStruct((8, 48, 128), jnp.bfloat16),
        in_specs=[in_vmem],
        out_specs=in_vmem,
        compiler_params=params,
        name="pack",
    )(conv_weight)
    blocks = lax.all_to_all(mine, "zt", 0, 0, tiled=True)

    shared = by_masks(features, DP)
    blocks, *shared = lax.optimization_barrier((blocks, *shared))

    blocks = everyone(blocks, SPREAD, 8).reshape(64, 48, 128)
    activated = pl.pallas_call(
        activate_kernel,
        out_shape=jax.ShapeDtypeStruct((4, rows, width), jnp.bfloat16),
        in_specs=[in_vmem] * 5,
        out_specs=in_vmem,
        compiler_params=params,
        name="activate",
    )(*shared, conv_gain[None])
    edge = jnp.where(zp == 0, activated[:, :2], activated[:, rows - 2 :])
    odd, even = range(1, 128, 2), range(0, 128, 2)
    steps = [
        [(i, i + step) for i in odd if i + step < 128] + [(i, i - step) for i in even if i - step >= 0]
        for step in (1, 2)
    ]
    other = swapped(activated, "zp")
    end, far_end = (lax.ppermute(edge, SEQ, step) for step in steps)
    wide = pl.pallas_call(
        expand_kernel,
        out_shape=jax.ShapeDtypeStruct((KW * width, 256), jnp.bfloat16),
        in_specs=[in_smem, in_vmem],
        out_specs=in_vmem,
        scratch_shapes=[pltpu.VMEM((KW * width, 256), jnp.float32)],
        compiler_params=params,
        name="expand",
    )(place, blocks)
    partial = pl.pallas_call(
        conv_kernel,
        out_shape=jax.ShapeDtypeStruct((8, 3 * rows // 2, 128), jnp.bfloat16),
        in_specs=[in_smem] + [in_vmem] * 5,
        out_specs=in_vmem,
        compiler_params=params,
        name="conv",
    )(place, activated, other, end, far_end, wide)
    partial = lax.all_to_all(partial, SHARE, 0, 0, tiled=True)

    stream, attn_in, packed = pl.pallas_call(
        stream_kernel,
        out_shape=[
            jax.ShapeDtypeStruct((rows, width), jnp.bfloat16),
            jax.ShapeDtypeStruct((8, rows, width), jnp.bfloat16),
            jax.ShapeDtypeStruct((5 * rows // 2, 128), jnp.bfloat16),
        ],
        in_specs=[in_vmem] * 5,
        out_specs=[in_vmem] * 3,
        compiler_params=params,
        name="stream",
    )(partial, features, attn_gain[None], key_weight, value_weight)
    asked = lax.all_to_all(attn_in, SPREAD, 0, 0, tiled=True)
    pairs = lax.all_gather(packed, COLUMN, axis=0)
    out = pl.pallas_call(
        functools.partial(attend_kernel, heads, size),
        out_shape=jax.ShapeDtypeStruct((8, rows, heads * value_size + STATS), jnp.bfloat16),
        in_specs=[in_vmem] * 3,
        out_specs=in_vmem,
        scratch_shapes=[
            pltpu.VMEM((8 * rows, heads * size), jnp.bfloat16),
            pltpu.VMEM((size, 16 * rows), jnp.bfloat16),
            pltpu.VMEM((16 * rows, 256), jnp.bfloat16),
            pltpu.VMEM((16 * rows, 256), jnp.bfloat16),
        ],
        compiler_params=params,
        name="attend",
    )(asked, query_weight, pairs)
    parts = lax.all_to_all(out, SPREAD, 0, 0, tiled=True)
    attended = pl.pallas_call(
        functools.partial(combine_kernel, heads),
        out_shape=jax.ShapeDtypeStruct((rows, heads * value_size), jnp.bfloat16),
        compiler_params=pltpu.CompilerParams(vmem_limit_bytes=32 * 1024 * 1024),
        name="combine",
    )(parts)
    return (stream, attended)


def solution(mesh):
    finer = Mesh(mesh.devices.reshape(SIZES), AXES)
    placed = (P(AXES, None), P(), P(SEQ, None), P(), P(), P(), P())
    return jax.shard_map(
        local,
        mesh=finer,
        in_specs=placed,
        out_specs=(P(AXES, None), P(AXES, None)),
        check_vma=False,
    )
```

```python
import functools

import jax
import jax.numpy as jnp
from jax import lax
from jax.experimental import pallas as pl
from jax.experimental.pallas import tpu as pltpu
from jax.sharding import Mesh
from jax.sharding import PartitionSpec as P

KW = 5
DP = ("xl", "co")
SEQ = ("xh", "y1", "y0", "zt", "zp")
AXES = DP + SEQ
SIZES = (2, 2, 2, 2, 2, 8, 2)
SHARE = ("xl", "co", "zp")
SPREAD = ("xh", "y1", "y0")
COLUMN = ("zt", "zp")
STATS = 128


def everyone(block, axes, count):
    sent = jnp.broadcast_to(block[None], (count,) + block.shape)
    return lax.all_to_all(sent, axes, 0, 0, tiled=True)


def swapped(block, axis):
    return lax.ppermute(block, axis, [(0, 1), (1, 0)])


def by_masks(block, axes):
    count = 2 ** len(axes)
    return [block] + [
        lax.ppermute(block, axes, [(i, i ^ mask) for i in range(count)]) for mask in range(1, count)
    ]


def normalize(values, gain):
    mean_square = jnp.mean(values * values, axis=-1, keepdims=True)
    return values * lax.rsqrt(mean_square + 1e-06) * gain


def pack_kernel(w_ref, out_ref):
    group = lax.axis_index(DP)
    depth = w_ref.shape[0]
    whole = w_ref[:, pl.ds(pl.multiple_of(group * 128, 128), 128)].astype(jnp.float32)
    tile = w_ref[:, pl.ds(pl.multiple_of(512 + (group // 2) * 128, 128), 128)].astype(jnp.float32)
    turned = pltpu.roll(tile, 64, 1)
    odd = group % 2 == 1
    left, right = jnp.where(odd, turned, tile), jnp.where(odd, tile, turned)
    half = depth // 2
    lane = lax.broadcasted_iota(jnp.int32, (half, 128), 1)
    rest = jnp.where(lane < 64, left[:half], right[half:])
    out = jnp.concatenate([whole, jnp.zeros((2, 128), jnp.float32), rest, jnp.zeros((1, 128), jnp.float32)])
    out = out.astype(jnp.bfloat16)
    for i in range(out_ref.shape[0]):
        out_ref[i] = out


def activate_kernel(x_ref, gain_ref, out_ref):
    for i in range(x_ref.shape[0]):
        values = normalize(x_ref[i].astype(jnp.float32), gain_ref[...])
        out_ref[i] = jax.nn.gelu(values, approximate=True).astype(jnp.bfloat16)


def expand_kernel(place_ref, w_ref, out_ref, wide_ref):
    zp = place_ref[1]
    count = w_ref.shape[0]
    depth = out_ref.shape[0] // (2 * count)
    wide_ref[...] = jnp.zeros_like(wide_ref)
    for side in range(2):

        @pl.when(zp == side)
        def _():
            for i in range(count):
                start = (2 * i + side) * depth
                block = w_ref[i].astype(jnp.float32)
                tail = block[32:48]
                wide_ref[start : start + depth, :128] = block[:depth]
                wide_ref[start : start + depth // 2, 128:] = tail[: depth // 2]
                wide_ref[start + depth // 2 : start + depth, 128:] = pltpu.roll(tail, 64, 1)[: depth // 2]

    out_ref[...] = wide_ref[...].astype(jnp.bfloat16)


def conv_kernel(place_ref, mine_ref, other_ref, end_ref, far_end_ref, wide_ref, out_ref):
    zp = place_ref[1]
    _, held, width = mine_ref.shape
    rows = 2 * held
    even = zp == 0
    mine, other = mine_ref[...], other_ref[...]
    first, second = jnp.where(even, mine, other), jnp.where(even, other, mine)
    x = jnp.concatenate([first, second], axis=1).reshape(4 * rows, width)
    end, far_end = end_ref[...].astype(jnp.float32), far_end_ref[...].astype(jnp.float32)
    before, after = jnp.where(even, end, far_end), jnp.where(even, far_end, end)
    ends = jnp.concatenate([before.reshape(8, width), after.reshape(8, width)]).astype(jnp.bfloat16)
    sums = [None] * 4
    for offset in range(KW):
        w = wide_ref[offset * width : (offset + 1) * width, :]
        y = jnp.dot(x, w, preferred_element_type=jnp.float32)
        z = jnp.dot(ends, w, preferred_element_type=jnp.float32)
        for part in range(4):
            body = y[part * rows : (part + 1) * rows]
            line = jnp.concatenate([z[2 * part : 2 * part + 2], body, z[8 + 2 * part : 10 + 2 * part]])
            term = line[offset : offset + rows]
            sums[part] = term if offset == 0 else sums[part] + term
    lane = lax.broadcasted_iota(jnp.int32, (held // 2, 128), 1)
    for part in range(4):
        rest = sums[part][:, 128:]
        turned = pltpu.roll(rest, 64, 1)
        for half in range(2):
            low, middle, high = half * held, half * held + held // 2, (half + 1) * held
            value = [sums[part][low:high, :128], jnp.where(lane < 64, rest[low:middle], turned[middle:high])]
            out_ref[2 * part + half] = jnp.concatenate(value).astype(jnp.bfloat16)


def stream_kernel(parts_ref, mine_ref, gain_ref, kw_ref, vw_ref, stream_ref, in_ref, pack_ref):
    inputs = mine_ref[...].astype(jnp.float32)
    rows = inputs.shape[0]
    lane = lax.broadcasted_iota(jnp.int32, (rows // 2, 128), 1)
    wholes, rests = [], []
    for j in range(4):
        total = parts_ref[2 * j].astype(jnp.float32) + parts_ref[2 * j + 1].astype(jnp.float32)
        wholes.append(total[:rows])
        rests.append((total[rows:], pltpu.roll(total[rows:], 64, 1)))
    tiles = [
        jnp.concatenate(
            [
                jnp.where(lane < 64, rests[j][0], rests[j + 1][1]),
                jnp.where(lane < 64, rests[j][1], rests[j + 1][0]),
            ]
        )
        for j in (0, 2)
    ]
    conv_out = jnp.concatenate(wholes + tiles, axis=1)
    stream = (inputs + conv_out).astype(jnp.bfloat16)
    stream_ref[...] = stream
    attn_in = normalize(stream.astype(jnp.float32), gain_ref[...]).astype(jnp.bfloat16)
    for i in range(in_ref.shape[0]):
        in_ref[i] = attn_in
    keys = jnp.dot(attn_in, kw_ref[...], preferred_element_type=jnp.float32)
    values = jnp.dot(attn_in, vw_ref[...], preferred_element_type=jnp.float32)
    tail = jnp.concatenate([values[: rows // 2, 128:], values[rows // 2 :, 128:]], axis=1)
    pack_ref[...] = jnp.concatenate([keys, values[:, :128], tail]).astype(jnp.bfloat16)


def unpack(ref, k_ref, ve_ref, vo_ref):
    lane = lax.broadcasted_iota(jnp.int32, (32, 128), 1)
    one = jnp.ones((32, 128), jnp.float32)
    count = ref.shape[0]
    keys = jnp.concatenate([ref[block, 0:64, :] for block in range(count)])
    k_ref[...] = keys.astype(jnp.float32).T.astype(jnp.bfloat16)
    for block in range(count):
        base = block * 64
        tail = ref[block, 128:160, :].astype(jnp.float32)
        turned = pltpu.roll(tail, 64, 1)
        for half in range(2):
            here = slice(base + 32 * half, base + 32 * half + 32)
            low = ref[block, 64 + 32 * half : 96 + 32 * half, :].astype(jnp.float32)
            shifted = pltpu.roll(low, 64, 1)
            left, right = (turned, tail) if half else (tail, turned)
            ve_ref[here, 0:128] = low.astype(jnp.bfloat16)
            ve_ref[here, 128:256] = jnp.where(lane < 64, left, one).astype(jnp.bfloat16)
            vo_ref[here, 0:128] = jnp.where(lane < 64, one, shifted).astype(jnp.bfloat16)
            vo_ref[here, 128:256] = jnp.where(lane < 64, shifted, right).astype(jnp.bfloat16)


def attend_kernel(heads, size, x_ref, qw_ref, pack_ref, out_ref, q_ref, k_ref, ve_ref, vo_ref):
    unpack(pack_ref, k_ref, ve_ref, vo_ref)
    blocks, block, width = x_ref.shape
    rows, chunk = blocks * block, 256
    q = jnp.dot(x_ref[...].reshape(rows, width), qw_ref[...], preferred_element_type=jnp.float32) * size ** (-0.5)
    q_ref[...] = q.astype(jnp.bfloat16)
    lane = lax.broadcasted_iota(jnp.int32, (chunk, 128), 1)
    def scores(start, head):
        q = q_ref[start : start + chunk, head * size : (head + 1) * size]
        return jnp.dot(q, k_ref[...], preferred_element_type=jnp.float32)

    def put(start, low, value):
        value = value.astype(jnp.bfloat16)
        for i in range(chunk // block):
            out_ref[start // block + i, :, low : low + 128] = value[i * block : (i + 1) * block]

    steps = [(start, head) for start in range(0, rows, chunk) for head in range(heads)]
    following = scores(*steps[0])
    for step, (start, head) in enumerate(steps):
        s = following
        if step + 1 < len(steps):
            following = scores(*steps[step + 1])
        peak = jnp.max(s, axis=-1, keepdims=True)
        p = jnp.exp(s - peak).astype(jnp.bfloat16)
        if head == 0:
            stats = jnp.zeros((chunk, STATS), jnp.float32)
        base = head // 2 * 384
        if head % 2 == 0:
            even = jnp.dot(p, ve_ref[...], preferred_element_type=jnp.float32)
            stats = jnp.where(lane == 72 + head, even[:, 128:], stats)
            stats = jnp.where(lane == 64 + head, peak, stats)
            put(start, base, even[:, :128])
        else:
            odd = jnp.dot(p, vo_ref[...], preferred_element_type=jnp.float32)
            stats = jnp.where(lane == 8 + head, odd[:, :128], stats)
            stats = jnp.where(lane == head, peak, stats)
            put(start, base + 128, jnp.where(lane < 64, even[:, 128:], odd[:, :128]))
            put(start, base + 256, odd[:, 128:])
        if head == heads - 1:
            first = stats.astype(jnp.bfloat16).astype(jnp.float32)
            rest = stats - first
            second = rest.astype(jnp.bfloat16).astype(jnp.float32)
            third = rest - second
            put(start, heads * 192, first + pltpu.roll(second, 16, 1) + pltpu.roll(third, 32, 1))


def combine_kernel(heads, parts_ref, out_ref):
    count, rows, _ = parts_ref.shape
    lane = lax.broadcasted_iota(jnp.int32, (rows, 128), 1)
    base = heads * 192
    parts = []
    for i in range(count):
        stats = parts_ref[i, :, base:].astype(jnp.float32)
        parts.append(stats + pltpu.roll(stats, STATS - 16, 1) + pltpu.roll(stats, STATS - 32, 1))
    top = functools.reduce(jnp.maximum, parts)
    scales = [jnp.exp(part - top) for part in parts]
    terms = [scale * pltpu.roll(part, STATS - 8, 1) for part, scale in zip(parts, scales)]
    inverse = 1.0 / functools.reduce(jnp.add, terms)
    shares = [scale * inverse for scale in scales]
    weights = []
    for head in range(heads):
        at = head if head % 2 else 64 + head
        weights.append([share[:, at : at + 1] for share in shares])
    for tile in range(heads * 192 // 128):
        low, high = tile * 128 // 192, (tile * 128 + 127) // 192
        total = jnp.zeros((rows, 128), jnp.float32)
        for i in range(count):
            weight = weights[low][i]
            if high != low:
                weight = jnp.where(lane < high * 192 - tile * 128, weight, weights[high][i])
            total = total + weight * parts_ref[i, :, tile * 128 : tile * 128 + 128].astype(jnp.float32)
        out_ref[:, tile * 128 : tile * 128 + 128] = total.astype(jnp.bfloat16)


def local(features, conv_gain, conv_weight, attn_gain, query_weight, key_weight, value_weight):
    rows, width = features.shape
    size = key_weight.shape[1]
    value_size = value_weight.shape[1]
    heads = query_weight.shape[1] // size
    zp = lax.axis_index("zp")
    place = jnp.stack([lax.axis_index(DP), zp])
    in_smem = pl.BlockSpec(memory_space=pltpu.SMEM)
    in_vmem = pl.BlockSpec(memory_space=pltpu.VMEM)
    params = pltpu.CompilerParams(vmem_limit_bytes=32 * 1024 * 1024)

    mine = pl.pallas_call(
        pack_kernel,
        out_shape=jax.ShapeDtypeStruct((8, 48, 128), jnp.bfloat16),
        in_specs=[in_vmem],
        out_specs=in_vmem,
        compiler_params=params,
        name="pack",
    )(conv_weight)
    blocks = lax.all_to_all(mine, "zt", 0, 0, tiled=True)

    shared = lax.all_gather(features, DP, axis=0)
    blocks, shared = lax.optimization_barrier((blocks, shared))

    blocks = everyone(blocks, SPREAD, 8).reshape(64, 48, 128)
    activated = pl.pallas_call(
        activate_kernel,
        out_shape=jax.ShapeDtypeStruct((4, rows, width), jnp.bfloat16),
        in_specs=[in_vmem] * 2,
        out_specs=in_vmem,
        compiler_params=params,
        name="activate",
    )(shared, conv_gain[None])
    edge = jnp.where(zp == 0, activated[:, :2], activated[:, rows - 2 :])
    odd, even = range(1, 128, 2), range(0, 128, 2)
    steps = [
        [(i, i + step) for i in odd if i + step < 128] + [(i, i - step) for i in even if i - step >= 0]
        for step in (1, 2)
    ]
    other = swapped(activated, "zp")
    end, far_end = (lax.ppermute(edge, SEQ, step) for step in steps)
    wide = pl.pallas_call(
        expand_kernel,
        out_shape=jax.ShapeDtypeStruct((KW * width, 256), jnp.bfloat16),
        in_specs=[in_smem, in_vmem],
        out_specs=in_vmem,
        scratch_shapes=[pltpu.VMEM((KW * width, 256), jnp.float32)],
        compiler_params=params,
        name="expand",
    )(place, blocks)
    partial = pl.pallas_call(
        conv_kernel,
        out_shape=jax.ShapeDtypeStruct((8, 3 * rows // 2, 128), jnp.bfloat16),
        in_specs=[in_smem] + [in_vmem] * 5,
        out_specs=in_vmem,
        compiler_params=params,
        name="conv",
    )(place, activated, other, end, far_end, wide)
    partial = lax.all_to_all(partial, SHARE, 0, 0, tiled=True)

    stream, attn_in, packed = pl.pallas_call(
        stream_kernel,
        out_shape=[
            jax.ShapeDtypeStruct((rows, width), jnp.bfloat16),
            jax.ShapeDtypeStruct((8, rows, width), jnp.bfloat16),
            jax.ShapeDtypeStruct((5 * rows // 2, 128), jnp.bfloat16),
        ],
        in_specs=[in_vmem] * 5,
        out_specs=[in_vmem] * 3,
        compiler_params=params,
        name="stream",
    )(partial, features, attn_gain[None], key_weight, value_weight)
    asked = lax.all_to_all(attn_in, SPREAD, 0, 0, tiled=True)
    pairs = lax.all_gather(packed, COLUMN, axis=0)
    out = pl.pallas_call(
        functools.partial(attend_kernel, heads, size),
        out_shape=jax.ShapeDtypeStruct((8, rows, heads * value_size + STATS), jnp.bfloat16),
        in_specs=[in_vmem] * 3,
        out_specs=in_vmem,
        scratch_shapes=[
            pltpu.VMEM((8 * rows, heads * size), jnp.bfloat16),
            pltpu.VMEM((size, 16 * rows), jnp.bfloat16),
            pltpu.VMEM((16 * rows, 256), jnp.bfloat16),
            pltpu.VMEM((16 * rows, 256), jnp.bfloat16),
        ],
        compiler_params=params,
        name="attend",
    )(asked, query_weight, pairs)
    parts = lax.all_to_all(out, SPREAD, 0, 0, tiled=True)
    attended = pl.pallas_call(
        functools.partial(combine_kernel, heads),
        out_shape=jax.ShapeDtypeStruct((rows, heads * value_size), jnp.bfloat16),
        compiler_params=pltpu.CompilerParams(vmem_limit_bytes=32 * 1024 * 1024),
        name="combine",
    )(parts)
    return (stream, attended)


def solution(mesh):
    finer = Mesh(mesh.devices.reshape(SIZES), AXES)
    placed = (P(AXES, None), P(), P(SEQ, None), P(), P(), P(), P())
    return jax.shard_map(
        local,
        mesh=finer,
        in_specs=placed,
        out_specs=(P(AXES, None), P(AXES, None)),
        check_vma=False,
    )
```

```python
import functools

import jax
import jax.numpy as jnp
from jax import lax
from jax.experimental import pallas as pl
from jax.experimental.pallas import tpu as pltpu
from jax.sharding import Mesh
from jax.sharding import PartitionSpec as P

KW = 5
DP = ("xl", "co")
SEQ = ("xh", "y1", "y0", "zt", "zp")
AXES = DP + SEQ
SIZES = (2, 2, 2, 2, 2, 8, 2)
SHARE = ("xl", "co", "zp")
SPREAD = ("xh", "y1", "y0")
COLUMN = ("zt", "zp")
STATS = 128


def everyone(block, axes, count):
    sent = jnp.broadcast_to(block[None], (count,) + block.shape)
    return lax.all_to_all(sent, axes, 0, 0, tiled=True)


def swapped(block, axis):
    return lax.ppermute(block, axis, [(0, 1), (1, 0)])


def by_masks(block, axes):
    count = 2 ** len(axes)
    return [block] + [
        lax.ppermute(block, axes, [(i, i ^ mask) for i in range(count)]) for mask in range(1, count)
    ]


def normalize(values, gain):
    mean_square = jnp.mean(values * values, axis=-1, keepdims=True)
    return values * lax.rsqrt(mean_square + 1e-06) * gain


def pack_kernel(w_ref, out_ref):
    group = lax.axis_index(DP)
    depth = w_ref.shape[0]
    whole = w_ref[:, pl.ds(pl.multiple_of(group * 128, 128), 128)].astype(jnp.float32)
    tile = w_ref[:, pl.ds(pl.multiple_of(512 + (group // 2) * 128, 128), 128)].astype(jnp.float32)
    turned = pltpu.roll(tile, 64, 1)
    odd = group % 2 == 1
    left, right = jnp.where(odd, turned, tile), jnp.where(odd, tile, turned)
    half = depth // 2
    lane = lax.broadcasted_iota(jnp.int32, (half, 128), 1)
    rest = jnp.where(lane < 64, left[:half], right[half:])
    out = jnp.concatenate([whole, jnp.zeros((2, 128), jnp.float32), rest, jnp.zeros((1, 128), jnp.float32)])
    out = out.astype(jnp.bfloat16)
    for i in range(out_ref.shape[0]):
        out_ref[i] = out


def activate_kernel(x_ref, gain_ref, out_ref):
    for i in range(x_ref.shape[0]):
        values = normalize(x_ref[i].astype(jnp.float32), gain_ref[...])
        out_ref[i] = jax.nn.gelu(values, approximate=True).astype(jnp.bfloat16)


def expand_kernel(place_ref, w_ref, out_ref):
    zp = place_ref[1]
    count = w_ref.shape[0]
    depth = out_ref.shape[0] // (2 * count)
    out_ref[...] = jnp.zeros_like(out_ref)
    for side in range(2):

        @pl.when(zp == side)
        def _():
            for i in range(count):
                start = (2 * i + side) * depth
                block = w_ref[i].astype(jnp.float32)
                tail = block[32:48]
                rest = jnp.concatenate([tail[: depth // 2], pltpu.roll(tail, 64, 1)[: depth // 2]])
                out_ref[start : start + depth, :128] = block[:depth].astype(jnp.bfloat16)
                out_ref[start : start + depth, 128:] = rest.astype(jnp.bfloat16)


def conv_kernel(place_ref, mine_ref, other_ref, end_ref, far_end_ref, wide_ref, out_ref, x_ref):
    zp = place_ref[1]
    _, held, width = mine_ref.shape
    rows = 2 * held
    even = zp == 0
    x_ref[:, pl.ds(pl.multiple_of(zp * held, held), held), :] = mine_ref[...]
    x_ref[:, pl.ds(pl.multiple_of((1 - zp) * held, held), held), :] = other_ref[...]
    x = x_ref[...].reshape(4 * rows, width)
    end, far_end = end_ref[...].astype(jnp.float32), far_end_ref[...].astype(jnp.float32)
    before, after = jnp.where(even, end, far_end), jnp.where(even, far_end, end)
    ends = jnp.concatenate([before.reshape(8, width), after.reshape(8, width)]).astype(jnp.bfloat16)
    sums = [None] * 4
    for offset in range(KW):
        w = wide_ref[offset * width : (offset + 1) * width, :]
        y = jnp.dot(x, w, preferred_element_type=jnp.float32)
        z = jnp.dot(ends, w, preferred_element_type=jnp.float32)
        for part in range(4):
            body = y[part * rows : (part + 1) * rows]
            line = jnp.concatenate([z[2 * part : 2 * part + 2], body, z[8 + 2 * part : 10 + 2 * part]])
            term = line[offset : offset + rows]
            sums[part] = term if offset == 0 else sums[part] + term
    lane = lax.broadcasted_iota(jnp.int32, (held // 2, 128), 1)
    for part in range(4):
        rest = sums[part][:, 128:]
        turned = pltpu.roll(rest, 64, 1)
        for half in range(2):
            low, middle, high = half * held, half * held + held // 2, (half + 1) * held
            value = [sums[part][low:high, :128], jnp.where(lane < 64, rest[low:middle], turned[middle:high])]
            out_ref[2 * part + half] = jnp.concatenate(value).astype(jnp.bfloat16)


def stream_kernel(parts_ref, mine_ref, gain_ref, kw_ref, vw_ref, stream_ref, in_ref, pack_ref):
    inputs = mine_ref[...].astype(jnp.float32)
    rows = inputs.shape[0]
    lane = lax.broadcasted_iota(jnp.int32, (rows // 2, 128), 1)
    wholes, rests = [], []
    for j in range(4):
        total = parts_ref[2 * j].astype(jnp.float32) + parts_ref[2 * j + 1].astype(jnp.float32)
        wholes.append(total[:rows])
        rests.append((total[rows:], pltpu.roll(total[rows:], 64, 1)))
    tiles = [
        jnp.concatenate(
            [
                jnp.where(lane < 64, rests[j][0], rests[j + 1][1]),
                jnp.where(lane < 64, rests[j][1], rests[j + 1][0]),
            ]
        )
        for j in (0, 2)
    ]
    conv_out = jnp.concatenate(wholes + tiles, axis=1)
    stream = (inputs + conv_out).astype(jnp.bfloat16)
    stream_ref[...] = stream
    attn_in = normalize(stream.astype(jnp.float32), gain_ref[...]).astype(jnp.bfloat16)
    for i in range(in_ref.shape[0]):
        in_ref[i] = attn_in
    keys = jnp.dot(attn_in, kw_ref[...], preferred_element_type=jnp.float32)
    values = jnp.dot(attn_in, vw_ref[...], preferred_element_type=jnp.float32)
    tail = jnp.concatenate([values[: rows // 2, 128:], values[rows // 2 :, 128:]], axis=1)
    pack_ref[...] = jnp.concatenate([keys, values[:, :128], tail]).astype(jnp.bfloat16)


def unpack(ref, k_ref, ve_ref, vo_ref):
    lane = lax.broadcasted_iota(jnp.int32, (32, 128), 1)
    one = jnp.ones((32, 128), jnp.float32)
    count = ref.shape[0]
    keys = jnp.concatenate([ref[block, 0:64, :] for block in range(count)])
    k_ref[...] = keys.astype(jnp.float32).T.astype(jnp.bfloat16)
    for block in range(count):
        base = block * 64
        tail = ref[block, 128:160, :].astype(jnp.float32)
        turned = pltpu.roll(tail, 64, 1)
        for half in range(2):
            here = slice(base + 32 * half, base + 32 * half + 32)
            low = ref[block, 64 + 32 * half : 96 + 32 * half, :].astype(jnp.float32)
            shifted = pltpu.roll(low, 64, 1)
            left, right = (turned, tail) if half else (tail, turned)
            ve_ref[here, 0:128] = low.astype(jnp.bfloat16)
            ve_ref[here, 128:256] = jnp.where(lane < 64, left, one).astype(jnp.bfloat16)
            vo_ref[here, 0:128] = jnp.where(lane < 64, one, shifted).astype(jnp.bfloat16)
            vo_ref[here, 128:256] = jnp.where(lane < 64, shifted, right).astype(jnp.bfloat16)


def attend_kernel(heads, size, x_ref, qw_ref, pack_ref, out_ref, q_ref, k_ref, ve_ref, vo_ref):
    unpack(pack_ref, k_ref, ve_ref, vo_ref)
    blocks, block, width = x_ref.shape
    rows, chunk = blocks * block, 256
    q = jnp.dot(x_ref[...].reshape(rows, width), qw_ref[...], preferred_element_type=jnp.float32) * size ** (-0.5)
    q_ref[...] = q.astype(jnp.bfloat16)
    lane = lax.broadcasted_iota(jnp.int32, (chunk, 128), 1)
    def scores(start, head):
        q = q_ref[start : start + chunk, head * size : (head + 1) * size]
        return jnp.dot(q, k_ref[...], preferred_element_type=jnp.float32)

    def put(start, low, value):
        value = value.astype(jnp.bfloat16)
        for i in range(chunk // block):
            out_ref[start // block + i, :, low : low + 128] = value[i * block : (i + 1) * block]

    steps = [(start, head) for start in range(0, rows, chunk) for head in range(heads)]
    following = scores(*steps[0])
    for step, (start, head) in enumerate(steps):
        s = following
        if step + 1 < len(steps):
            following = scores(*steps[step + 1])
        peak = jnp.max(s, axis=-1, keepdims=True)
        p = jnp.exp(s - peak).astype(jnp.bfloat16)
        if head == 0:
            stats = jnp.zeros((chunk, STATS), jnp.float32)
        base = head // 2 * 384
        if head % 2 == 0:
            even = jnp.dot(p, ve_ref[...], preferred_element_type=jnp.float32)
            stats = jnp.where(lane == 72 + head, even[:, 128:], stats)
            stats = jnp.where(lane == 64 + head, peak, stats)
            put(start, base, even[:, :128])
        else:
            odd = jnp.dot(p, vo_ref[...], preferred_element_type=jnp.float32)
            stats = jnp.where(lane == 8 + head, odd[:, :128], stats)
            stats = jnp.where(lane == head, peak, stats)
            put(start, base + 128, jnp.where(lane < 64, even[:, 128:], odd[:, :128]))
            put(start, base + 256, odd[:, 128:])
        if head == heads - 1:
            first = stats.astype(jnp.bfloat16).astype(jnp.float32)
            rest = stats - first
            second = rest.astype(jnp.bfloat16).astype(jnp.float32)
            third = rest - second
            put(start, heads * 192, first + pltpu.roll(second, 16, 1) + pltpu.roll(third, 32, 1))


def combine_kernel(heads, parts_ref, out_ref):
    count, rows, _ = parts_ref.shape
    lane = lax.broadcasted_iota(jnp.int32, (rows, 128), 1)
    base = heads * 192
    parts = []
    for i in range(count):
        stats = parts_ref[i, :, base:].astype(jnp.float32)
        parts.append(stats + pltpu.roll(stats, STATS - 16, 1) + pltpu.roll(stats, STATS - 32, 1))
    top = functools.reduce(jnp.maximum, parts)
    scales = [jnp.exp(part - top) for part in parts]
    terms = [scale * pltpu.roll(part, STATS - 8, 1) for part, scale in zip(parts, scales)]
    inverse = 1.0 / functools.reduce(jnp.add, terms)
    shares = [scale * inverse for scale in scales]
    weights = []
    for head in range(heads):
        at = head if head % 2 else 64 + head
        weights.append([share[:, at : at + 1] for share in shares])
    for tile in range(heads * 192 // 128):
        low, high = tile * 128 // 192, (tile * 128 + 127) // 192
        total = jnp.zeros((rows, 128), jnp.float32)
        for i in range(count):
            weight = weights[low][i]
            if high != low:
                weight = jnp.where(lane < high * 192 - tile * 128, weight, weights[high][i])
            total = total + weight * parts_ref[i, :, tile * 128 : tile * 128 + 128].astype(jnp.float32)
        out_ref[:, tile * 128 : tile * 128 + 128] = total.astype(jnp.bfloat16)


def local(features, conv_gain, conv_weight, attn_gain, query_weight, key_weight, value_weight):
    rows, width = features.shape
    size = key_weight.shape[1]
    value_size = value_weight.shape[1]
    heads = query_weight.shape[1] // size
    zp = lax.axis_index("zp")
    place = jnp.stack([lax.axis_index(DP), zp])
    in_smem = pl.BlockSpec(memory_space=pltpu.SMEM)
    in_vmem = pl.BlockSpec(memory_space=pltpu.VMEM)
    params = pltpu.CompilerParams(vmem_limit_bytes=32 * 1024 * 1024)

    mine = pl.pallas_call(
        pack_kernel,
        out_shape=jax.ShapeDtypeStruct((8, 48, 128), jnp.bfloat16),
        in_specs=[in_vmem],
        out_specs=in_vmem,
        compiler_params=params,
        name="pack",
    )(conv_weight)
    blocks = lax.all_to_all(mine, "zt", 0, 0, tiled=True)

    shared = lax.all_gather(features, DP, axis=0)

    activated = pl.pallas_call(
        activate_kernel,
        out_shape=jax.ShapeDtypeStruct((4, rows, width), jnp.bfloat16),
        in_specs=[in_vmem] * 2,
        out_specs=in_vmem,
        compiler_params=params,
        name="activate",
    )(shared, conv_gain[None])
    blocks, activated = lax.optimization_barrier((blocks, activated))
    blocks = everyone(blocks, SPREAD, 8).reshape(64, 48, 128)
    edge = jnp.where(zp == 0, activated[:, :2], activated[:, rows - 2 :])
    odd, even = range(1, 128, 2), range(0, 128, 2)
    steps = [
        [(i, i + step) for i in odd if i + step < 128] + [(i, i - step) for i in even if i - step >= 0]
        for step in (2, 1)
    ]
    other = swapped(activated, "zp")
    far_end, end = (lax.ppermute(edge, SEQ, step) for step in steps)
    wide = pl.pallas_call(
        expand_kernel,
        out_shape=jax.ShapeDtypeStruct((KW * width, 256), jnp.bfloat16),
        in_specs=[in_smem, in_vmem],
        out_specs=in_vmem,
        compiler_params=params,
        name="expand",
    )(place, blocks)
    partial = pl.pallas_call(
        conv_kernel,
        out_shape=jax.ShapeDtypeStruct((8, 3 * rows // 2, 128), jnp.bfloat16),
        in_specs=[in_smem] + [in_vmem] * 5,
        out_specs=in_vmem,
        scratch_shapes=[pltpu.VMEM((4, 2 * rows, width), jnp.bfloat16)],
        compiler_params=params,
        name="conv",
    )(place, activated, other, end, far_end, wide)
    partial = lax.all_to_all(partial, SHARE, 0, 0, tiled=True)

    stream, attn_in, packed = pl.pallas_call(
        stream_kernel,
        out_shape=[
            jax.ShapeDtypeStruct((rows, width), jnp.bfloat16),
            jax.ShapeDtypeStruct((8, rows, width), jnp.bfloat16),
            jax.ShapeDtypeStruct((5 * rows // 2, 128), jnp.bfloat16),
        ],
        in_specs=[in_vmem] * 5,
        out_specs=[in_vmem] * 3,
        compiler_params=params,
        name="stream",
    )(partial, features, attn_gain[None], key_weight, value_weight)
    asked = lax.all_to_all(attn_in, SPREAD, 0, 0, tiled=True)
    pairs = lax.all_gather(packed, COLUMN, axis=0)
    out = pl.pallas_call(
        functools.partial(attend_kernel, heads, size),
        out_shape=jax.ShapeDtypeStruct((8, rows, heads * value_size + STATS), jnp.bfloat16),
        in_specs=[in_vmem] * 3,
        out_specs=in_vmem,
        scratch_shapes=[
            pltpu.VMEM((8 * rows, heads * size), jnp.bfloat16),
            pltpu.VMEM((size, 16 * rows), jnp.bfloat16),
            pltpu.VMEM((16 * rows, 256), jnp.bfloat16),
            pltpu.VMEM((16 * rows, 256), jnp.bfloat16),
        ],
        compiler_params=params,
        name="attend",
    )(asked, query_weight, pairs)
    parts = lax.all_to_all(out, SPREAD, 0, 0, tiled=True)
    attended = pl.pallas_call(
        functools.partial(combine_kernel, heads),
        out_shape=jax.ShapeDtypeStruct((rows, heads * value_size), jnp.bfloat16),
        compiler_params=pltpu.CompilerParams(vmem_limit_bytes=32 * 1024 * 1024),
        name="combine",
    )(parts)
    return (stream, attended)


def solution(mesh):
    finer = Mesh(mesh.devices.reshape(SIZES), AXES)
    placed = (P(AXES, None), P(), P(SEQ, None), P(), P(), P(), P())
    return jax.shard_map(
        local,
        mesh=finer,
        in_specs=placed,
        out_specs=(P(AXES, None), P(AXES, None)),
        check_vma=False,
    )
```

```python
import functools

import jax
import jax.numpy as jnp
from jax import lax
from jax.experimental import pallas as pl
from jax.experimental.pallas import tpu as pltpu
from jax.sharding import Mesh
from jax.sharding import PartitionSpec as P

KW = 5
DP = ("xl", "co")
SEQ = ("xh", "y1", "y0", "zt", "zp")
AXES = DP + SEQ
SIZES = (2, 2, 2, 2, 2, 8, 2)
SHARE = ("xl", "co", "zp")
SPREAD = ("xh", "y1", "y0")
COLUMN = ("zt", "zp")
STATS = 128


def everyone(block, axes, count):
    sent = jnp.broadcast_to(block[None], (count,) + block.shape)
    return lax.all_to_all(sent, axes, 0, 0, tiled=True)


def swapped(block, axis):
    return lax.ppermute(block, axis, [(0, 1), (1, 0)])


def by_masks(block, axes):
    count = 2 ** len(axes)
    return [block] + [
        lax.ppermute(block, axes, [(i, i ^ mask) for i in range(count)]) for mask in range(1, count)
    ]


def normalize(values, gain):
    mean_square = jnp.mean(values * values, axis=-1, keepdims=True)
    return values * lax.rsqrt(mean_square + 1e-06) * gain


def pack_kernel(w_ref, out_ref):
    group = lax.axis_index(DP)
    depth = w_ref.shape[0]
    whole = w_ref[:, pl.ds(pl.multiple_of(group * 128, 128), 128)].astype(jnp.float32)
    tile = w_ref[:, pl.ds(pl.multiple_of(512 + (group // 2) * 128, 128), 128)].astype(jnp.float32)
    turned = pltpu.roll(tile, 64, 1)
    odd = group % 2 == 1
    left, right = jnp.where(odd, turned, tile), jnp.where(odd, tile, turned)
    half = depth // 2
    lane = lax.broadcasted_iota(jnp.int32, (half, 128), 1)
    rest = jnp.where(lane < 64, left[:half], right[half:])
    out = jnp.concatenate([whole, jnp.zeros((2, 128), jnp.float32), rest, jnp.zeros((1, 128), jnp.float32)])
    out = out.astype(jnp.bfloat16)
    for i in range(out_ref.shape[0]):
        out_ref[i] = out


def activate_kernel(x_ref, gain_ref, out_ref):
    for i in range(x_ref.shape[0]):
        values = normalize(x_ref[i].astype(jnp.float32), gain_ref[...])
        out_ref[i] = jax.nn.gelu(values, approximate=True).astype(jnp.bfloat16)


def expand_kernel(place_ref, w_ref, out_ref):
    zp = place_ref[1]
    count = w_ref.shape[0]
    depth = out_ref.shape[0] // (2 * count)
    out_ref[...] = jnp.zeros_like(out_ref)
    for side in range(2):

        @pl.when(zp == side)
        def _():
            for i in range(count):
                start = (2 * i + side) * depth
                block = w_ref[i].astype(jnp.float32)
                tail = block[32:48]
                rest = jnp.concatenate([tail[: depth // 2], pltpu.roll(tail, 64, 1)[: depth // 2]])
                out_ref[start : start + depth, :128] = block[:depth].astype(jnp.bfloat16)
                out_ref[start : start + depth, 128:] = rest.astype(jnp.bfloat16)


def conv_kernel(place_ref, mine_ref, other_ref, end_ref, far_end_ref, wide_ref, out_ref, x_ref):
    zp = place_ref[1]
    _, held, width = mine_ref.shape
    rows = 2 * held
    even = zp == 0
    for part in range(4):
        x_ref[pl.ds(pl.multiple_of(part * rows + zp * held, held), held), :] = mine_ref[part]
        x_ref[pl.ds(pl.multiple_of(part * rows + (1 - zp) * held, held), held), :] = other_ref[part]
    end, far_end = end_ref[...].astype(jnp.float32), far_end_ref[...].astype(jnp.float32)
    before, after = jnp.where(even, end, far_end), jnp.where(even, far_end, end)
    ends = jnp.concatenate([before.reshape(8, width), after.reshape(8, width)]).astype(jnp.bfloat16)
    x_ref[4 * rows :, :] = ends
    x = x_ref[...]
    sums = [None] * 4
    for offset in range(KW):
        w = wide_ref[offset * width : (offset + 1) * width, :]
        y = jnp.dot(x, w, preferred_element_type=jnp.float32)
        z = y[4 * rows :]
        for part in range(4):
            body = y[part * rows : (part + 1) * rows]
            line = jnp.concatenate([z[2 * part : 2 * part + 2], body, z[8 + 2 * part : 10 + 2 * part]])
            term = line[offset : offset + rows]
            sums[part] = term if offset == 0 else sums[part] + term
    lane = lax.broadcasted_iota(jnp.int32, (held // 2, 128), 1)
    for part in range(4):
        rest = sums[part][:, 128:]
        turned = pltpu.roll(rest, 64, 1)
        for half in range(2):
            low, middle, high = half * held, half * held + held // 2, (half + 1) * held
            value = [sums[part][low:high, :128], jnp.where(lane < 64, rest[low:middle], turned[middle:high])]
            out_ref[2 * part + half] = jnp.concatenate(value).astype(jnp.bfloat16)


def stream_kernel(parts_ref, mine_ref, gain_ref, kw_ref, vw_ref, stream_ref, in_ref, pack_ref):
    inputs = mine_ref[...].astype(jnp.float32)
    rows = inputs.shape[0]
    lane = lax.broadcasted_iota(jnp.int32, (rows // 2, 128), 1)
    wholes, rests = [], []
    for j in range(4):
        total = parts_ref[2 * j].astype(jnp.float32) + parts_ref[2 * j + 1].astype(jnp.float32)
        wholes.append(total[:rows])
        rests.append((total[rows:], pltpu.roll(total[rows:], 64, 1)))
    tiles = [
        jnp.concatenate(
            [
                jnp.where(lane < 64, rests[j][0], rests[j + 1][1]),
                jnp.where(lane < 64, rests[j][1], rests[j + 1][0]),
            ]
        )
        for j in (0, 2)
    ]
    conv_out = jnp.concatenate(wholes + tiles, axis=1)
    stream = (inputs + conv_out).astype(jnp.bfloat16)
    stream_ref[...] = stream
    attn_in = normalize(stream.astype(jnp.float32), gain_ref[...]).astype(jnp.bfloat16)
    for i in range(in_ref.shape[0]):
        in_ref[i] = attn_in
    keys = jnp.dot(attn_in, kw_ref[...], preferred_element_type=jnp.float32)
    values = jnp.dot(attn_in, vw_ref[...], preferred_element_type=jnp.float32)
    tail = jnp.concatenate([values[: rows // 2, 128:], values[rows // 2 :, 128:]], axis=1)
    pack_ref[...] = jnp.concatenate([keys, values[:, :128], tail]).astype(jnp.bfloat16)


def unpack(ref, k_ref, ve_ref, vo_ref):
    lane = lax.broadcasted_iota(jnp.int32, (32, 128), 1)
    one = jnp.ones((32, 128), jnp.float32)
    count = ref.shape[0]
    keys = jnp.concatenate([ref[block, 0:64, :] for block in range(count)])
    k_ref[...] = keys.astype(jnp.float32).T.astype(jnp.bfloat16)
    for block in range(count):
        base = block * 64
        tail = ref[block, 128:160, :].astype(jnp.float32)
        turned = pltpu.roll(tail, 64, 1)
        for half in range(2):
            here = slice(base + 32 * half, base + 32 * half + 32)
            low = ref[block, 64 + 32 * half : 96 + 32 * half, :].astype(jnp.float32)
            shifted = pltpu.roll(low, 64, 1)
            left, right = (turned, tail) if half else (tail, turned)
            ve_ref[here, 0:128] = low.astype(jnp.bfloat16)
            ve_ref[here, 128:256] = jnp.where(lane < 64, left, one).astype(jnp.bfloat16)
            vo_ref[here, 0:128] = jnp.where(lane < 64, one, shifted).astype(jnp.bfloat16)
            vo_ref[here, 128:256] = jnp.where(lane < 64, shifted, right).astype(jnp.bfloat16)


def attend_kernel(heads, size, x_ref, qw_ref, pack_ref, out_ref, q_ref, k_ref, ve_ref, vo_ref):
    unpack(pack_ref, k_ref, ve_ref, vo_ref)
    blocks, block, width = x_ref.shape
    rows, chunk = blocks * block, 256
    q = jnp.dot(x_ref[...].reshape(rows, width), qw_ref[...], preferred_element_type=jnp.float32) * size ** (-0.5)
    q_ref[...] = q.astype(jnp.bfloat16)
    lane = lax.broadcasted_iota(jnp.int32, (chunk, 128), 1)
    def scores(start, head):
        q = q_ref[start : start + chunk, head * size : (head + 1) * size]
        return jnp.dot(q, k_ref[...], preferred_element_type=jnp.float32)

    def put(start, low, value):
        value = value.astype(jnp.bfloat16)
        for i in range(chunk // block):
            out_ref[start // block + i, :, low : low + 128] = value[i * block : (i + 1) * block]

    steps = [(start, head) for start in range(0, rows, chunk) for head in range(heads)]
    following = scores(*steps[0])
    for step, (start, head) in enumerate(steps):
        s = following
        if step + 1 < len(steps):
            following = scores(*steps[step + 1])
        peak = jnp.max(s, axis=-1, keepdims=True)
        p = jnp.exp(s - peak).astype(jnp.bfloat16)
        if head == 0:
            stats = jnp.zeros((chunk, STATS), jnp.float32)
        base = head // 2 * 384
        if head % 2 == 0:
            even = jnp.dot(p, ve_ref[...], preferred_element_type=jnp.float32)
            stats = jnp.where(lane == 72 + head, even[:, 128:], stats)
            stats = jnp.where(lane == 64 + head, peak, stats)
            put(start, base, even[:, :128])
        else:
            odd = jnp.dot(p, vo_ref[...], preferred_element_type=jnp.float32)
            stats = jnp.where(lane == 8 + head, odd[:, :128], stats)
            stats = jnp.where(lane == head, peak, stats)
            put(start, base + 128, jnp.where(lane < 64, even[:, 128:], odd[:, :128]))
            put(start, base + 256, odd[:, 128:])
        if head == heads - 1:
            first = stats.astype(jnp.bfloat16).astype(jnp.float32)
            rest = stats - first
            second = rest.astype(jnp.bfloat16).astype(jnp.float32)
            third = rest - second
            put(start, heads * 192, first + pltpu.roll(second, 16, 1) + pltpu.roll(third, 32, 1))


def combine_kernel(heads, parts_ref, out_ref):
    count, rows, _ = parts_ref.shape
    lane = lax.broadcasted_iota(jnp.int32, (rows, 128), 1)
    base = heads * 192
    parts = []
    for i in range(count):
        stats = parts_ref[i, :, base:].astype(jnp.float32)
        parts.append(stats + pltpu.roll(stats, STATS - 16, 1) + pltpu.roll(stats, STATS - 32, 1))
    top = functools.reduce(jnp.maximum, parts)
    scales = [jnp.exp(part - top) for part in parts]
    terms = [scale * pltpu.roll(part, STATS - 8, 1) for part, scale in zip(parts, scales)]
    inverse = 1.0 / functools.reduce(jnp.add, terms)
    shares = [scale * inverse for scale in scales]
    weights = []
    for head in range(heads):
        at = head if head % 2 else 64 + head
        weights.append([share[:, at : at + 1] for share in shares])
    for tile in range(heads * 192 // 128):
        low, high = tile * 128 // 192, (tile * 128 + 127) // 192
        total = jnp.zeros((rows, 128), jnp.float32)
        for i in range(count):
            weight = weights[low][i]
            if high != low:
                weight = jnp.where(lane < high * 192 - tile * 128, weight, weights[high][i])
            total = total + weight * parts_ref[i, :, tile * 128 : tile * 128 + 128].astype(jnp.float32)
        out_ref[:, tile * 128 : tile * 128 + 128] = total.astype(jnp.bfloat16)


def local(features, conv_gain, conv_weight, attn_gain, query_weight, key_weight, value_weight):
    rows, width = features.shape
    size = key_weight.shape[1]
    value_size = value_weight.shape[1]
    heads = query_weight.shape[1] // size
    zp = lax.axis_index("zp")
    place = jnp.stack([lax.axis_index(DP), zp])
    in_smem = pl.BlockSpec(memory_space=pltpu.SMEM)
    in_vmem = pl.BlockSpec(memory_space=pltpu.VMEM)
    params = pltpu.CompilerParams(vmem_limit_bytes=32 * 1024 * 1024)

    mine = pl.pallas_call(
        pack_kernel,
        out_shape=jax.ShapeDtypeStruct((8, 48, 128), jnp.bfloat16),
        in_specs=[in_vmem],
        out_specs=in_vmem,
        compiler_params=params,
        name="pack",
    )(conv_weight)
    blocks = lax.all_to_all(mine, "zt", 0, 0, tiled=True)

    shared = lax.all_gather(features, DP, axis=0)

    activated = pl.pallas_call(
        activate_kernel,
        out_shape=jax.ShapeDtypeStruct((4, rows, width), jnp.bfloat16),
        in_specs=[in_vmem] * 2,
        out_specs=in_vmem,
        compiler_params=params,
        name="activate",
    )(shared, conv_gain[None])
    blocks, activated = lax.optimization_barrier((blocks, activated))
    blocks = everyone(blocks, SPREAD, 8).reshape(64, 48, 128)
    edge = jnp.where(zp == 0, activated[:, :2], activated[:, rows - 2 :])
    odd, even = range(1, 128, 2), range(0, 128, 2)
    steps = [
        [(i, i + step) for i in odd if i + step < 128] + [(i, i - step) for i in even if i - step >= 0]
        for step in (2, 1)
    ]
    other = swapped(activated, "zp")
    far_end, end = (lax.ppermute(edge, SEQ, step) for step in steps)
    wide = pl.pallas_call(
        expand_kernel,
        out_shape=jax.ShapeDtypeStruct((KW * width, 256), jnp.bfloat16),
        in_specs=[in_smem, in_vmem],
        out_specs=in_vmem,
        compiler_params=params,
        name="expand",
    )(place, blocks)
    partial = pl.pallas_call(
        conv_kernel,
        out_shape=jax.ShapeDtypeStruct((8, 3 * rows // 2, 128), jnp.bfloat16),
        in_specs=[in_smem] + [in_vmem] * 5,
        out_specs=in_vmem,
        scratch_shapes=[pltpu.VMEM((8 * rows + 16, width), jnp.bfloat16)],
        compiler_params=params,
        name="conv",
    )(place, activated, other, end, far_end, wide)
    partial = lax.all_to_all(partial, SHARE, 0, 0, tiled=True)

    stream, attn_in, packed = pl.pallas_call(
        stream_kernel,
        out_shape=[
            jax.ShapeDtypeStruct((rows, width), jnp.bfloat16),
            jax.ShapeDtypeStruct((8, rows, width), jnp.bfloat16),
            jax.ShapeDtypeStruct((5 * rows // 2, 128), jnp.bfloat16),
        ],
        in_specs=[in_vmem] * 5,
        out_specs=[in_vmem] * 3,
        compiler_params=params,
        name="stream",
    )(partial, features, attn_gain[None], key_weight, value_weight)
    asked = lax.all_to_all(attn_in, SPREAD, 0, 0, tiled=True)
    pairs = lax.all_gather(packed, COLUMN, axis=0)
    out = pl.pallas_call(
        functools.partial(attend_kernel, heads, size),
        out_shape=jax.ShapeDtypeStruct((8, rows, heads * value_size + STATS), jnp.bfloat16),
        in_specs=[in_vmem] * 3,
        out_specs=in_vmem,
        scratch_shapes=[
            pltpu.VMEM((8 * rows, heads * size), jnp.bfloat16),
            pltpu.VMEM((size, 16 * rows), jnp.bfloat16),
            pltpu.VMEM((16 * rows, 256), jnp.bfloat16),
            pltpu.VMEM((16 * rows, 256), jnp.bfloat16),
        ],
        compiler_params=params,
        name="attend",
    )(asked, query_weight, pairs)
    parts = lax.all_to_all(out, SPREAD, 0, 0, tiled=True)
    attended = pl.pallas_call(
        functools.partial(combine_kernel, heads),
        out_shape=jax.ShapeDtypeStruct((rows, heads * value_size), jnp.bfloat16),
        compiler_params=pltpu.CompilerParams(vmem_limit_bytes=32 * 1024 * 1024),
        name="combine",
    )(parts)
    return (stream, attended)


def solution(mesh):
    finer = Mesh(mesh.devices.reshape(SIZES), AXES)
    placed = (P(AXES, None), P(), P(SEQ, None), P(), P(), P(), P())
    return jax.shard_map(
        local,
        mesh=finer,
        in_specs=placed,
        out_specs=(P(AXES, None), P(AXES, None)),
        check_vma=False,
    )
```
